128 devices in a mesh: seq: 32 (over y_lo, x, z), head: 4 (over y_hi, core).
Axes of the slice: x: 4, y: 4 (y_hi: 2, y_lo: 2; y = y_hi * 2 + y_lo), z: 4, core: 2. Of those that a mesh axis runs over, the one named last changes fastest.
Arguments:
- tokens: bfloat16 [16384, 4096], P('seq'), may hold values from -15 to 15
- mask_flags: int32 [16384], P('seq'), may hold values 0 or 1
- mask_embed: bfloat16 [4096], replicated, may hold values from -5 to 5
- w_query: bfloat16 [4096, 2048], P(None, 'head'), as said below
- w_key: bfloat16 [4096, 2048], P(None, 'head'), as said below
- w_value: bfloat16 [4096, 2048], P(None, 'head'), may hold values from -0.375 to 0.375
- w_out: bfloat16 [2048, 4096], P('head'), may hold values from -0.125 to 0.125
Outputs:
- mixed_rows: bfloat16 [16384, 4096], P(('seq', 'head'))
The draws below stay inside these ranges and needn't reach their ends.
Inputs may be any that keep to these rules, and one draw needn't show every extreme that they name: `w_query`: entries of order one over the square root of 4096. `w_key`: entries of order one over the square root of 4096.
All inputs are finite; a program needn't handle non-finite values. No bound on the sum of `mask_flags` on one device may be relied on, other than what follows from the above.
Results may differ from the reference program's by a relative error of at most 0.015.
Values may be sent and summed in bfloat16 or wider, within the bound.
A program may use at most 384 MiB of HBM per device.

```python
import math
import jax
import jax.numpy as jnp
from jax import lax

D = 4096
DH = 128
HEADS = 16
TOKENS = 16384


def shared_weight(key):
    return jnp.clip(jax.random.normal(key, (D, HEADS * DH), jnp.float32), -5.0, 5.0)


def draw_w_query(key, part):
    shared = shared_weight(key)
    return (shared * (2.0 / D) ** 0.5).astype(jnp.bfloat16)


def draw_w_key(key, part):
    shared = shared_weight(key)
    key = jax.random.fold_in(key, 12)
    own_part = jnp.clip(jax.random.normal(key, (D, HEADS * DH), jnp.float32), -5.0, 5.0)
    return ((0.2 * shared + 0.9798 * own_part) * (2.0 / D) ** 0.5).astype(jnp.bfloat16)


def draw_tokens(key, part):
    key = jax.random.fold_in(key, 13)
    drawn = jnp.clip(jax.random.normal(key, (TOKENS, D), jnp.float32), -5.0, 5.0)
    return drawn.astype(jnp.bfloat16)


def plant(values, rng, least, high):
    longest = values.shape.index(max(values.shape))
    spots = []
    for shift in (0, 1):
        where = [jax.random.randint(jax.random.fold_in(rng, axis), (), 0, length) for axis, length in enumerate(values.shape)]
        where[longest] = (where[longest] + shift) % values.shape[longest]
        spots.append(tuple(where))
    return values.at[spots[0]].set(least).at[spots[1]].set(high)


def shard_levels(rng, shape, cuts, smallest, top_value):
    def one(position, shards_of):
        steps = jax.random.uniform(jax.random.fold_in(jax.random.fold_in(rng, 6), position), (shards_of,), jnp.float32, smallest / len(cuts), top_value / len(cuts))
        return jnp.repeat(jnp.exp(steps), shape[position] // shards_of).reshape((-1,) + (1,) * (len(shape) - position - 1))

    factor_of = one(*cuts[0])
    for cut in cuts[1:]:
        factor_of = factor_of * one(*cut)
    return factor_of


def centred(key, shape, deviation, most, shards=(), dtype=jnp.bfloat16):
    values = deviation * jax.random.normal(key, shape, jnp.float32)
    if shards:
        values = values * shard_levels(key, shape, shards, -0.22, 0.18)
    return jnp.clip(values, -most, most).astype(dtype)


def setup_inputs(seed: int = 0) -> dict:
    key_list = jax.random.split(jax.random.key(seed), 8)
    return {
        "tokens": draw_tokens(jax.random.fold_in(key_list[7], 71), 0),
        "mask_flags": plant((jax.random.randint(key_list[1], (TOKENS,), 0, 2) < 1).astype(jnp.int32), jax.random.fold_in(key_list[1], 1), 0, 1),
        "mask_embed": centred(key_list[2], (D,), 1.0, 5.0),
        "w_query": draw_w_query(jax.random.fold_in(key_list[7], 71), 0),
        "w_key": draw_w_key(jax.random.fold_in(key_list[7], 71), 0),
        "w_value": centred(key_list[5], (D, HEADS * DH), (D // 16) ** -0.5, 0.375, ((1, 4),)),
        "w_out": centred(key_list[6], (HEADS * DH, D), (HEADS * DH) ** -0.5, 0.125, ((0, 4),)),
    }


def rotate(values, positions, head_size):
    halfway = head_size // 2
    indices = jnp.arange(halfway).astype(jnp.float32)
    frequency = jnp.exp(indices * (-2.0 * math.log(500000.0) / head_size))
    angles = positions[:, None] * frequency[None, :]
    cosine = jnp.cos(angles)[:, None, :]
    sine_table = jnp.sin(angles)[:, None, :]
    shaped = values.reshape(values.shape[0], -1, head_size)
    leading = shaped[..., :halfway]
    trailing = shaped[..., halfway:]
    turned = jnp.concatenate([leading * cosine - trailing * sine_table, trailing * cosine + leading * sine_table], axis=-1)
    return turned.reshape(values.shape)


def reference(tokens, mask_flags, mask_embed, w_query, w_key, w_value, w_out):
    mask_rows = mask_flags.astype(jnp.float32)[:, None]
    hidden = (tokens.astype(jnp.float32) + mask_rows * mask_embed.astype(jnp.float32)[None, :]).astype(jnp.bfloat16)
    positions = jnp.arange(TOKENS).astype(jnp.float32)
    queries = rotate(jnp.dot(hidden, w_query, preferred_element_type=jnp.float32), positions, DH).astype(jnp.bfloat16)
    key_rows = rotate(jnp.dot(hidden, w_key, preferred_element_type=jnp.float32), positions, DH).astype(jnp.bfloat16)
    value_rows = jnp.dot(hidden, w_value, preferred_element_type=jnp.float32).astype(jnp.bfloat16)
    block_rows = min(256, TOKENS)
    query_blocks = queries.reshape(TOKENS // block_rows, block_rows, HEADS, DH)
    key_heads = key_rows.reshape(TOKENS, HEADS, DH).astype(jnp.float32)
    value_heads = value_rows.reshape(TOKENS, HEADS, DH).astype(jnp.float32)
    score_scale = DH ** -0.5

    def attend(query_block):
        scores = jnp.einsum("qhd,khd->hqk", query_block.astype(jnp.float32), key_heads) * score_scale
        row_peak = jnp.max(scores, axis=-1, keepdims=True)
        weights = jnp.exp(scores - row_peak)
        row_total = jnp.sum(weights, axis=-1)
        rounded = lax.optimization_barrier(weights.astype(jnp.bfloat16)).astype(jnp.float32)
        summed = jnp.einsum("hqk,khd->qhd", rounded, value_heads)
        return (summed / row_total.T[:, :, None]).astype(jnp.bfloat16)

    attention = lax.map(attend, query_blocks).reshape(TOKENS, HEADS * DH)
    return jnp.dot(attention, w_out, preferred_element_type=jnp.float32).astype(jnp.bfloat16)
```

```python
import functools
import math

import jax
import jax.numpy as jnp
from jax import lax
from jax.experimental import pallas as pl
from jax.experimental.pallas import tpu as pltpu
from jax.sharding import PartitionSpec as P

DH = 128
MESH = pl.DeviceIdType.MESH
F32 = jnp.float32
BF16 = jnp.bfloat16
VMEM_BYTES = 58 * 2**20
TOTAL_LOW = 2.0**-60
TOTAL_HIGH = 2.0**100

OWN = {(0, d): d + (d + 3) // 4 for d in range(4)}
SIB = {(0, 0): 1, (0, 1): 5, (0, 2): 6, (0, 3): 7}
for _d in range(4):
    OWN[1, _d], OWN[3, _d], SIB[1, _d], SIB[3, _d] = (8 + 4 * _d + n for n in range(4))
    OWN[2, _d] = 24 + 4 * (_d // 2) + _d % 2
    SIB[2, _d] = OWN[2, _d] + 2
OWN_OF = {slot: key for key, slot in OWN.items()}


def place():
    seq, head = lax.axis_index("seq"), lax.axis_index("head")
    y_lo, x, z = seq // 16, (seq // 4) % 4, seq % 4
    y_hi, core = head // 2, head % 2
    return y_lo, x, z, y_hi, core


def seq_of(y_lo, x, z):
    return y_lo * 16 + x * 4 + z


def remote(src, dst, send_sem, recv_sem, seq, head):
    return pltpu.make_async_remote_copy(
        src_ref=src, dst_ref=dst, send_sem=send_sem, recv_sem=recv_sem,
        device_id=(seq, head), device_id_type=MESH,
    )


def lanes(blocks):
    return jnp.concatenate([blocks[n] for n in range(blocks.shape[0])], axis=1)


def turned_blocks(rows):
    return jnp.concatenate(
        [rows[n * DH:(n + 1) * DH].T for n in range(rows.shape[0] // DH)], axis=0
    )


def attend_kernel(
    tok_hbm, flags_ref, embed_ref, cos_ref, sin_ref, wq_hbm, wk_hbm, wv_hbm, wo_hbm,
    o_ref, total_ref, q_out, kv_out, wg_out,
    tok_v, w_v, pacc, stq, stkv, qb, kvb, acc,
    load_sem, q_send, q_recv, a_send, kv_recv, f_send, dump_sem,
    wx_send, wx_recv, wz_send, wz_recv, ws_send, ws_recv,
):
    y_lo, x, z, y_hi, core = place()
    seq, head = seq_of(y_lo, x, z), y_hi * 2 + core
    sib = y_hi * 2 + (1 - core)
    straight = core == y_lo
    x_up, x_down = seq_of(y_lo, (x + 1) % 4, z), seq_of(y_lo, (x + 3) % 4, z)
    z_up, z_down = seq_of(y_lo, x, (z + 1) % 4), seq_of(y_lo, x, (z + 3) % 4)
    cross_seq, cross_head = seq_of(1 - y_lo, x, z), (1 - y_hi) * 2 + core

    pltpu.make_async_copy(tok_hbm, tok_v, load_sem.at[6]).start()
    far = 1 - z // 2
    near = z // 2
    order = [(wq_hbm, far), (wq_hbm, near), (wk_hbm, far), (wv_hbm, far), (wk_hbm, near), (wv_hbm, near)]

    def w_load(n):
        w, pair = order[n]
        cols = pl.ds(pl.multiple_of(pair * 256, 256), 256)
        return pltpu.make_async_copy(w.at[:, cols], w_v.at[n], load_sem.at[n])

    for n in range(6):
        w_load(n).start()

    barrier = pltpu.get_barrier_semaphore()

    def greet(s, h):
        pl.semaphore_signal(barrier, inc=1, device_id=(s, h), device_id_type=MESH)

    for i in range(4):
        @pl.when(jnp.logical_not(jnp.logical_and(straight, z == i)))
        def _():
            greet(seq_of(core, x, i), y_hi * 2 + y_lo)
    for s, h in ((x_up, head), (x_down, head), (z_up, head), (z_down, head), (seq, sib), (cross_seq, cross_head)):
        greet(s, h)

    @pl.when(straight)
    def _():
        pl.semaphore_wait(barrier, 9)

    @pl.when(jnp.logical_not(straight))
    def _():
        pl.semaphore_wait(barrier, 10)

    mine, theirs = (z % 2) * 256, (1 - z % 2) * 256

    def w_rows(base, k):
        return pl.ds(pl.multiple_of(base + 64 * k, 64), 64)

    def w_cross(k):
        return remote(wo_hbm.at[w_rows(mine, k)], wg_out.at[1, w_rows(mine, k)],
                      wx_send.at[k], wx_recv.at[k], cross_seq, cross_head)

    def w_side(k):
        to = z_up if k < 2 else z_down
        return remote(wg_out.at[1, w_rows(mine, k)], wg_out.at[1, w_rows(mine, k)],
                      wz_send.at[k], wz_recv.at[k], to, head)

    def w_side_in(k):
        return remote(wg_out.at[1, w_rows(theirs, k)], wg_out.at[1, w_rows(theirs, k)],
                      wz_send.at[k], wz_recv.at[k], z_up, head)

    def w_sib(n):
        if n == 8:
            return remote(wo_hbm, wg_out.at[0], ws_send.at[8], ws_recv.at[8], seq, sib)
        rows = w_rows(mine if n < 4 else theirs, n % 4)
        return remote(wg_out.at[1, rows], wg_out.at[2, rows], ws_send.at[n], ws_recv.at[n], seq, sib)

    def w_cross_in(k):
        w_cross(k).wait_recv()
        w_side(k).start()
        w_sib(k).start()

    for k in range(4):
        w_cross(k).start()

    pltpu.make_async_copy(tok_hbm, tok_v, load_sem.at[6]).wait()
    flag_cols = jnp.broadcast_to(flags_ref[...].astype(F32), (DH, flags_ref.shape[1])).T

    def add_embed(n, _):
        cols = pl.ds(pl.multiple_of(n * DH, DH), DH)
        added = embed_ref[:, cols].astype(F32)
        tok_v[:, cols] = (tok_v[:, cols].astype(F32) + flag_cols * added).astype(BF16)
        return 0

    lax.fori_loop(0, tok_v.shape[1] // DH, add_embed, 0)

    def rope(rows):
        return rows * cos_ref[...] + pltpu.roll(rows, DH // 2, 1) * sin_ref[...]

    def piece(n, e):
        return order_pair(n) * 2 + e

    def order_pair(n):
        return order[n][1]

    def a2a_q(m, pair, e):
        i = pair * 2 + e
        args = (stq.at[m], qb.at[z], q_send.at[m], q_recv.at[z])
        return remote(*args, seq_of(core, x, i), y_hi * 2 + y_lo), pltpu.make_async_copy(
            stq.at[m], qb.at[z], q_recv.at[z]), jnp.logical_and(straight, z == i)

    def a2a_kv(m, pair, e):
        i = pair * 2 + e
        d = (z - i + 4) % 4
        slot = d + (d + 3) // 4
        return remote(stkv.at[m], kvb.at[slot], a_send.at[m], kv_recv.at[slot],
                      seq_of(core, x, i), y_hi * 2 + y_lo), pltpu.make_async_copy(
            stkv.at[m], kvb.at[slot], kv_recv.at[slot]), jnp.logical_and(straight, z == i)

    def launch(copies):
        far_copy, own_copy, own = copies

        @pl.when(own)
        def _():
            own_copy.start()

        @pl.when(jnp.logical_not(own))
        def _():
            far_copy.start()

    def drain(copies):
        far_copy, _, own = copies

        @pl.when(jnp.logical_not(own))
        def _():
            far_copy.wait_send()

    score_scale = DH ** -0.5 * math.log2(math.e)
    for n in range(6):
        w_load(n).wait()
        pacc[...] = jnp.zeros_like(pacc)

        def multiply(k, _, n=n):
            depth = pl.ds(pl.multiple_of(k * 512, 512), 512)
            pacc[...] += jnp.dot(tok_v[:, depth], w_v[n, depth, :], preferred_element_type=F32)
            return 0

        lax.fori_loop(0, tok_v.shape[1] // 512, multiply, 0)
        pair = order[n][1]
        for e in range(2):
            rows = pacc[:, e * DH:(e + 1) * DH]
            if n < 2:
                m = n * 2 + e
                stq[m] = turned_blocks((rope(rows) * score_scale).astype(BF16))
                launch(a2a_q(m, pair, e))
            else:
                m = (n - 2) // 2 * 2 + e
                if n % 2 == 0:
                    stkv[m, 0] = rope(rows).astype(BF16)
                else:
                    stkv[m, 1] = turned_blocks(rows.astype(BF16))
                    launch(a2a_kv(m, pair, e))

    acc[...] = jnp.zeros_like(acc)
    total_ref[...] = jnp.zeros_like(total_ref)
    for j in range(4):
        remote(qb.at[j], qb.at[j], q_send.at[0], q_recv.at[j], seq, sib).wait_recv()
    q_dump = pltpu.make_async_copy(qb, q_out, dump_sem.at[16])
    q_dump.start()

    sends = []

    def forward(slot, to_slot, s, h):
        def copy():
            return remote(kvb.at[slot], kvb.at[to_slot], f_send.at[n_send], kv_recv.at[to_slot], s, h)
        n_send = len(sends)
        sends.append(copy)
        copy().start()

    def arrived(slot):
        remote(kvb.at[slot], kvb.at[slot], f_send.at[0], kv_recv.at[slot], seq, sib).wait_recv()
        if slot not in OWN_OF:
            return
        dx, d = OWN_OF[slot]
        if dx == 0:
            forward(slot, OWN[1, d], x_up, head)
            forward(slot, OWN[3, d], x_down, head)
        if dx == 1 and d % 2 == 0:
            forward(slot, OWN[2, d], x_up, head)
        if dx == 3 and d % 2 == 1:
            forward(slot, OWN[2, d], x_down, head)
        forward(slot, SIB[dx, d], seq, sib)

    extra = {
        2: lambda: w_cross_in(0),
        4: lambda: w_sib(8).start(),
        5: lambda: (w_side_in(0).wait_recv(), w_sib(4).start()),
        7: lambda: w_cross_in(1),
        10: lambda: (w_side_in(1).wait_recv(), w_sib(5).start()),
        12: lambda: w_cross_in(2),
        15: lambda: (w_side_in(2).wait_recv(), w_sib(6).start()),
    }
    blocks = qb.shape[0]

    def step(t, _):
        for k in range(16):
            @pl.when(t == k)
            def _(k=k):
                arrived(2 * k)
                arrived(2 * k + 1)
                if k in extra:
                    extra[k]()

        pltpu.make_async_copy(kvb.at[pl.ds(2 * t, 2)], kv_out.at[pl.ds(2 * t, 2)], dump_sem.at[t]).start()
        keys = kvb[pl.ds(2 * t, 2), 0].reshape(1024, DH)
        values = lanes(kvb[pl.ds(2 * t, 2), 1].reshape(8, DH, DH))

        def scores(i):
            return jnp.dot(keys, lanes(qb[i].reshape(4, DH, DH)), preferred_element_type=F32)

        now = scores(0)
        for i in range(blocks):
            later = scores(i + 1) if i + 1 < blocks else None
            cols = slice(i * 512, (i + 1) * 512)
            weights = jnp.exp2(now)
            total_ref[:, cols] += jnp.sum(weights.reshape(128, 8, 512), axis=0)
            acc[:, cols] += jnp.dot(values, weights.astype(BF16), preferred_element_type=F32)
            now = later
        return 0

    lax.fori_loop(0, 16, step, 0)

    w_cross_in(3)
    for i in range(blocks):
        cols = slice(i * 512, (i + 1) * 512)
        total = jnp.sum(total_ref[:, cols], axis=0, keepdims=True)
        done = (acc[:, cols] / total).astype(BF16)
        for n in range(4):
            o_ref[i * 512 + n * DH:i * 512 + (n + 1) * DH, :] = done[:, n * DH:(n + 1) * DH].T
    w_side_in(3).wait_recv()
    w_sib(7).start()

    for n in range(9):
        w_sib(n).wait_recv()
        w_sib(n).wait_send()
    for k in range(4):
        w_cross(k).wait_send()
        w_side(k).wait_send()
    for n in range(2):
        for e in range(2):
            drain(a2a_q(n * 2 + e, order[n][1], e))
            drain(a2a_kv(n * 2 + e, order[2 + 2 * n][1], e))
    for copy in sends:
        copy().wait_send()
    q_dump.wait()

    def dumped(t, _):
        pltpu.make_async_copy(kvb.at[pl.ds(2 * t, 2)], kv_out.at[pl.ds(2 * t, 2)], dump_sem.at[t]).wait()
        return 0

    lax.fori_loop(0, 16, dumped, 0)


def repair_kernel(total_ref, q_hbm, kv_hbm, o_in, o_hbm, qb, kv, acc, peak, total, o_v, sem):
    sums = jnp.sum(total_ref[...], axis=0, keepdims=True)
    good = jnp.logical_and(sums > TOTAL_LOW, sums < TOTAL_HIGH)
    bad = jnp.max(jnp.where(good, 0.0, 1.0))

    @pl.when(bad > 0.5)
    def _():
        load = pltpu.make_async_copy(q_hbm, qb, sem)
        load.start()
        load.wait()
        acc[...] = jnp.zeros_like(acc)
        total[...] = jnp.zeros_like(total)
        peak[...] = jnp.full_like(peak, -3e38)

        def chunk(n, _):
            load = pltpu.make_async_copy(kv_hbm.at[n], kv, sem)
            load.start()
            load.wait()

            def block(i, _):
                cols = pl.ds(pl.multiple_of(i * 512, 512), 512)
                scores = jnp.dot(kv[0], lanes(qb[i].reshape(4, DH, DH)), preferred_element_type=F32)
                old = peak[0:1, cols]
                new = jnp.maximum(old, jnp.max(scores, axis=0, keepdims=True))
                factor = jnp.exp2(old - new)
                weights = jnp.exp2(scores - new)
                peak[0:1, cols] = new
                total[0:1, cols] = total[0:1, cols] * factor + jnp.sum(weights, axis=0, keepdims=True)
                acc[:, cols] = acc[:, cols] * factor + jnp.dot(
                    lanes(kv[1].reshape(4, DH, DH)), weights.astype(BF16), preferred_element_type=F32
                )
                return 0

            lax.fori_loop(0, 4, block, 0)
            return 0

        lax.fori_loop(0, kv_hbm.shape[0], chunk, 0)
        for n in range(16):
            cols = slice(n * DH, (n + 1) * DH)
            o_v[cols, :] = (acc[:, cols] / total[0:1, cols]).astype(BF16).T
        store = pltpu.make_async_copy(o_v, o_hbm, sem)
        store.start()
        store.wait()


def out_kernel(o_ref, wo_hbm, wg_hbm, out_ref, full, w_v, load_sem, send_sem, recv_sem):
    y_lo, x, z, y_hi, core = place()
    straight = core == y_lo
    groups = [(wo_hbm, y_hi * 2 + core), (wg_hbm.at[0], y_hi * 2 + 1 - core),
              (wg_hbm.at[1], (1 - y_hi) * 2 + core), (wg_hbm.at[2], (1 - y_hi) * 2 + 1 - core)]
    loads = [pltpu.make_async_copy(src, w_v.at[g], load_sem.at[n]) for n, (src, g) in enumerate(groups)]
    for load in loads:
        load.start()

    barrier = pltpu.get_barrier_semaphore()
    for hi in range(2):
        for lo in range(2):
            for zz in range(4):
                same = (straight, y_hi == hi, y_lo == lo, z == zz)

                @pl.when(jnp.logical_not(functools.reduce(jnp.logical_and, same)))
                def _(hi=hi, lo=lo, zz=zz):
                    pl.semaphore_signal(barrier, inc=1, device_id=(seq_of(lo, x, zz), hi * 2 + y_lo), device_id_type=MESH)

    @pl.when(straight)
    def _():
        pl.semaphore_wait(barrier, 15)

    @pl.when(jnp.logical_not(straight))
    def _():
        pl.semaphore_wait(barrier, 16)

    mine = y_hi * 8 + y_lo * 4 + z
    copies = []
    for dz in range(4):
        for hi in range(2):
            for c in range(2):
                zz = (z + dz) % 4
                n = (dz * 2 + hi) * 2 + c
                own = functools.reduce(jnp.logical_and, (straight, y_hi == hi, core == c, dz == 0)) if dz == 0 else None
                rows = pl.ds(pl.multiple_of(zz * 512 + hi * 256 + c * 128, 128), 128)
                far = remote(o_ref.at[rows], full.at[mine], send_sem.at[n], recv_sem.at[mine],
                             seq_of(core, x, zz), hi * 2 + c)
                near = pltpu.make_async_copy(o_ref.at[rows], full.at[mine], recv_sem.at[mine])
                copies.append((far, near, own))
    for far, near, own in copies:
        if own is None:
            far.start()
        else:
            pl.when(own)(near.start)
            pl.when(jnp.logical_not(own))(far.start)
    for load in loads:
        load.wait()
    for n in range(16):
        remote(full.at[n], full.at[n], send_sem.at[0], recv_sem.at[n], seq_of(y_lo, x, z), y_hi * 2 + 1 - core).wait_recv()
    attention = [lanes(full[4 * g:4 * g + 4]) for g in range(4)]

    def columns(n, _):
        cols = pl.ds(pl.multiple_of(n * 512, 512), 512)
        total = jnp.dot(attention[0], w_v[0, :, cols], preferred_element_type=F32)
        for g in range(1, 4):
            total += jnp.dot(attention[g], w_v[g, :, cols], preferred_element_type=F32)
        out_ref[:, cols] = total.astype(BF16)
        return 0

    lax.fori_loop(0, out_ref.shape[1] // 512, columns, 0)
    for far, near, own in copies:
        if own is None:
            far.wait_send()
        else:
            pl.when(jnp.logical_not(own))(far.wait_send)


def rope_tables(rows):
    halfway = DH // 2
    frequency = jnp.exp(jnp.arange(halfway).astype(F32) * (-2.0 * math.log(500000.0) / DH))
    positions = (lax.axis_index("seq") * rows + jnp.arange(rows)).astype(F32)
    angles = positions[:, None] * frequency[None, :]
    cosine, sine = jnp.cos(angles), jnp.sin(angles)
    return jnp.concatenate([cosine, cosine], axis=1), jnp.concatenate([-sine, sine], axis=1)


def shards(tokens, mask_flags, mask_embed, w_query, w_key, w_value, w_out):
    rows, width = tokens.shape
    cosine, sine = rope_tables(rows)
    vmem, hbm = pl.BlockSpec(memory_space=pltpu.VMEM), pl.BlockSpec(memory_space=pl.ANY)
    dma = pltpu.SemaphoreType.DMA
    struct = jax.ShapeDtypeStruct
    attention, total, q_all, kv_all, w_all = pl.pallas_call(
        attend_kernel,
        out_shape=(
            struct((4 * rows, DH), BF16), struct((8, 4 * rows), F32), struct((4, rows, DH), BF16),
            struct((32, 2, rows, DH), BF16), struct((3,) + w_out.shape, BF16),
        ),
        in_specs=[hbm, vmem, vmem, vmem, vmem, hbm, hbm, hbm, hbm],
        out_specs=(vmem, vmem, hbm, hbm, hbm),
        scratch_shapes=[
            pltpu.VMEM((rows, width), BF16),
            pltpu.VMEM((6, width, 256), BF16),
            pltpu.VMEM((rows, 256), F32),
            pltpu.VMEM((4, rows, DH), BF16),
            pltpu.VMEM((4, 2, rows, DH), BF16),
            pltpu.VMEM((4, rows, DH), BF16),
            pltpu.VMEM((32, 2, rows, DH), BF16),
            pltpu.VMEM((DH, 4 * rows), F32),
            dma((7,)), dma((4,)), dma((4,)), dma((4,)), dma((32,)), dma((28,)), dma((17,)),
            dma((4,)), dma((4,)), dma((4,)), dma((4,)), dma((9,)), dma((9,)),
        ],
        compiler_params=pltpu.CompilerParams(
            collective_id=0, has_side_effects=True, vmem_limit_bytes=VMEM_BYTES
        ),
        name="attend",
    )(tokens, mask_flags.reshape(1, rows), mask_embed.reshape(1, width), cosine, sine, w_query, w_key, w_value, w_out)
    attention = pl.pallas_call(
        repair_kernel,
        out_shape=struct((4 * rows, DH), BF16),
        in_specs=[vmem, hbm, hbm, hbm],
        out_specs=hbm,
        scratch_shapes=[
            pltpu.VMEM((4, rows, DH), BF16),
            pltpu.VMEM((2, rows, DH), BF16),
            pltpu.VMEM((DH, 4 * rows), F32),
            pltpu.VMEM((8, 4 * rows), F32),
            pltpu.VMEM((8, 4 * rows), F32),
            pltpu.VMEM((4 * rows, DH), BF16),
            dma,
        ],
        input_output_aliases={3: 0},
        compiler_params=pltpu.CompilerParams(vmem_limit_bytes=VMEM_BYTES),
        name="repair",
    )(total, q_all, kv_all, attention)
    return pl.pallas_call(
        out_kernel,
        out_shape=struct((rows // 4, width), BF16),
        in_specs=[vmem, hbm, hbm],
        out_specs=vmem,
        scratch_shapes=[
            pltpu.VMEM((16, DH, DH), BF16),
            pltpu.VMEM((4,) + w_out.shape, BF16),
            dma((4,)), dma((16,)), dma((16,)),
        ],
        compiler_params=pltpu.CompilerParams(
            collective_id=1, has_side_effects=True, vmem_limit_bytes=VMEM_BYTES
        ),
        name="project_out",
    )(attention, w_out, w_all)


def solution(mesh):
    placed = (
        P("seq", None),
        P("seq"),
        P(),
        P(None, "head"),
        P(None, "head"),
        P(None, "head"),
        P("head", None),
    )
    return jax.shard_map(
        shards, mesh=mesh, in_specs=placed, out_specs=P(("seq", "head"), None), check_vma=False
    )
```

```python
import functools
import math

import jax
import jax.numpy as jnp
from jax import lax
from jax.experimental import pallas as pl
from jax.experimental.pallas import tpu as pltpu
from jax.sharding import PartitionSpec as P

DH = 128
MESH = pl.DeviceIdType.MESH
F32 = jnp.float32
BF16 = jnp.bfloat16
VMEM_BYTES = 58 * 2**20
TOTAL_LOW = 2.0**-60
TOTAL_HIGH = 2.0**100

USE = (
    ("own", 0, 0), ("sib", 0, 0), ("own", 1, 0), ("own", 3, 0), ("sib", 1, 0), ("sib", 3, 0),
    ("own", 0, 1), ("sib", 0, 1), ("own", 0, 3), ("own", 0, 2), ("sib", 0, 3), ("sib", 0, 2),
    ("own", 1, 1), ("own", 3, 1), ("sib", 1, 1), ("sib", 3, 1), ("own", 1, 3), ("own", 3, 3), ("sib", 1, 3), ("sib", 3, 3),
    ("own", 2, 0), ("own", 2, 1), ("sib", 2, 0), ("sib", 2, 1), ("own", 1, 2), ("own", 3, 2), ("sib", 1, 2), ("sib", 3, 2),
    ("own", 2, 3), ("own", 2, 2), ("sib", 2, 3), ("sib", 2, 2),
)
OWN = {(dx, e): n for n, (by, dx, e) in enumerate(USE) if by == "own"}
SIB = {(dx, e): n for n, (by, dx, e) in enumerate(USE) if by == "sib"}
EARLY = {1: ((0, 1),), 3: ((0, 3),)}
OWN_OF = {slot: key for key, slot in OWN.items()}

ORDER = (("kv", 0), ("q", 0), ("q", 1), ("kv", 1), ("kv", 3), ("kv", 2))
CROSS = (0, 1, 2, 3, 6, 7)
EXTRA = {
    0: (("own", 0),), 4: (("in", 0), ("in", 1)), 5: (("in", 2),), 6: (("in", 3),), 8: (("in", 4),), 9: (("in", 6),),
    10: (("in", 5), ("side", 0), ("side", 1)), 11: (("side", 2),), 12: (("in", 7), ("side", 3)), 13: (("side", 4),),
    14: (("side", 5),), 15: (("side", 6),), 16: (("side", 7),),
}


def place():
    seq, head = lax.axis_index("seq"), lax.axis_index("head")
    y_lo, x, z = seq // 16, (seq // 4) % 4, seq % 4
    y_hi, core = head // 2, head % 2
    return y_lo, x, z, y_hi, core


def seq_of(y_lo, x, z):
    return y_lo * 16 + x * 4 + z


def remote(src, dst, send_sem, recv_sem, seq, head):
    return pltpu.make_async_remote_copy(
        src_ref=src, dst_ref=dst, send_sem=send_sem, recv_sem=recv_sem,
        device_id=(seq, head), device_id_type=MESH,
    )


def lanes(blocks):
    return jnp.concatenate([blocks[n] for n in range(blocks.shape[0])], axis=1)


def turned_blocks(rows):
    return jnp.concatenate(
        [rows[n * DH:(n + 1) * DH].T for n in range(rows.shape[0] // DH)], axis=0
    )


def attend_kernel(
    tok_hbm, flags_ref, embed_ref, wq_hbm, wk_hbm, wv_hbm, wo_hbm,
    o_ref, total_ref, q_out, kv_out, wg_out,
    tok_v, w_v, pacc, cos_v, sin_v, stq, stkv, qb, kvb, acc,
    load_sem, q_send, q_recv, a_send, kv_recv, f_send, dump_sem,
    wx_send, wy_send, wx_recv, wz_send, wz_recv, ws_send, ws_recv,
):
    y_lo, x, z, y_hi, core = place()
    seq, head = seq_of(y_lo, x, z), y_hi * 2 + core
    sib = y_hi * 2 + (1 - core)
    straight = core == y_lo
    rows_here = tok_hbm.shape[0]
    x_up, x_down = seq_of(y_lo, (x + 1) % 4, z), seq_of(y_lo, (x + 3) % 4, z)
    z_up, z_down = seq_of(y_lo, x, (z + 1) % 4), seq_of(y_lo, x, (z + 3) % 4)
    y_seq = seq_of(1 - y_lo, x, z)
    cross_head = (1 - y_hi) * 2 + core

    def swapped(e):
        return 2 * ((z // 2 + e // 2) % 2) + (z % 2 + e % 2) % 2

    tok_load = pltpu.make_async_copy(tok_hbm, tok_v.at[pl.ds(0, rows_here)], load_sem.at[6])
    tok_load.start()
    for n, (kind, which) in enumerate(ORDER):
        if kind == "q":
            cols = pl.ds(pl.multiple_of(swapped(2 * which) // 2 * 256, 256), 256)
            pltpu.make_async_copy(wq_hbm.at[:, cols], w_v.at[n], load_sem.at[n]).start()
        else:
            cols = pl.ds(pl.multiple_of(swapped(which) * DH, DH), DH)
            pltpu.make_async_copy(wk_hbm.at[:, cols], w_v.at[n, :, pl.ds(0, DH)], load_sem.at[n]).start()
            pltpu.make_async_copy(wv_hbm.at[:, cols], w_v.at[n, :, pl.ds(DH, DH)], load_sem.at[n]).start()

    barrier = pltpu.get_barrier_semaphore()

    def greet(s, h):
        pl.semaphore_signal(barrier, inc=1, device_id=(s, h), device_id_type=MESH)

    for i in range(4):
        @pl.when(jnp.logical_not(jnp.logical_and(straight, z == i)))
        def _():
            greet(seq_of(core, x, i), y_hi * 2 + y_lo)
    for s, h in ((x_up, head), (x_down, head), (z_up, head), (z_down, head),
                 (seq, sib), (y_seq, head), (y_seq, cross_head)):
        greet(s, h)

    lane = lax.broadcasted_iota(jnp.int32, (1, DH), 1)
    frequency = jnp.exp((lane % (DH // 2)).astype(F32) * (-2.0 * math.log(500000.0) / DH))
    sign = jnp.where(lane < DH // 2, -1.0, 1.0)

    def angle_rows(n, _):
        rows = pl.ds(pl.multiple_of(n * 64, 64), 64)
        position = (lax.broadcasted_iota(jnp.int32, (64, DH), 0) + (seq * rows_here + n * 64)).astype(F32)
        angle = position * frequency
        cos_v[rows, :] = jnp.cos(angle)
        sin_v[rows, :] = jnp.sin(angle) * sign
        return 0

    lax.fori_loop(0, rows_here // 64, angle_rows, 0)

    @pl.when(straight)
    def _():
        pl.semaphore_wait(barrier, 10)

    @pl.when(jnp.logical_not(straight))
    def _():
        pl.semaphore_wait(barrier, 11)

    def w_chunk(colour_y, colour_z, q):
        base = (colour_y * 2 + colour_z) * 128 + 32 * (q % 4)
        return pl.ds(pl.multiple_of(base, 32), 32)

    def w_rows(q, y=None, z_par=None):
        y = y_lo if y is None else y
        z_par = z % 2 if z_par is None else z_par
        return w_chunk(y if q < 4 else 1 - y, z_par, q)

    def w_cross(n):
        rows = w_rows(CROSS[n], y=1 - y_lo)
        return remote(wo_hbm.at[rows], wg_out.at[1, rows], wx_send.at[n], wx_recv.at[CROSS[n]], y_seq, cross_head)

    def w_y(q):
        rows = w_rows(q)
        return remote(wg_out.at[1, rows], wg_out.at[1, rows], wy_send.at[q], wx_recv.at[q + 4], y_seq, head)

    def w_z(q, rows=None):
        rows = w_rows(q) if rows is None else rows
        return remote(wg_out.at[1, rows], wg_out.at[1, rows], wz_send.at[q], wz_recv.at[q],
                      z_up if q % 2 == 0 else z_down, head)

    def w_sib(n):
        if n == 16:
            return remote(wo_hbm, wg_out.at[0], ws_send.at[16], ws_recv.at[16], seq, sib)
        rows = w_rows(n) if n < 8 else w_rows(n - 8, z_par=1 - z % 2)
        return remote(wg_out.at[1, rows], wg_out.at[2, rows], ws_send.at[n], ws_recv.at[n], seq, sib)

    def w_arrived(q):
        rows = w_rows(q)
        remote(wg_out.at[1, rows], wg_out.at[1, rows], wx_send.at[0], wx_recv.at[q], y_seq, head).wait_recv()
        if q < 2:
            w_y(q).start()
        w_z(q).start()
        w_sib(q).start()

    def w_side(q):
        w_z(q, w_rows(q, z_par=1 - z % 2)).wait_recv()
        w_sib(8 + q).start()

    for n in range(len(CROSS)):
        w_cross(n).start()

    flag_cols = jnp.broadcast_to(flags_ref[...].astype(F32), (DH, rows_here)).T
    width = tok_v.shape[1]
    tok_v[rows_here:, :] = jnp.broadcast_to(embed_ref[...].reshape(1, width), (16, width))
    tok_load.wait()

    def rope(rows):
        return rows * cos_v[...] + pltpu.roll(rows, DH // 2, 1) * sin_v[...]

    def q_piece(m, i):
        return (remote(stq.at[m], qb.at[z], q_send.at[m], q_recv.at[z], seq_of(core, x, i), y_hi * 2 + y_lo),
                pltpu.make_async_copy(stq.at[m], qb.at[z], q_recv.at[z]))

    def kv_piece(high, low, i):
        slot = low * (1 - high) * OWN[0, 1] + high * (OWN[0, 2] + low * (OWN[0, 3] - OWN[0, 2]))
        m = 2 * high + low
        return (remote(stkv.at[m], kvb.at[slot], a_send.at[m], kv_recv.at[slot],
                       seq_of(core, x, i), y_hi * 2 + y_lo),
                pltpu.make_async_copy(stkv.at[m], kvb.at[slot], kv_recv.at[slot]))

    def launch(there, here, i):
        own = jnp.logical_and(straight, z == i)
        pl.when(own)(here.start)
        pl.when(jnp.logical_not(own))(there.start)

    def among(n, picks):
        return functools.reduce(jnp.logical_or, [n == p for p in picks])

    score_scale = DH ** -0.5 * math.log2(math.e)
    q_steps = [n for n, (kind, _) in enumerate(ORDER) if kind == "q"]
    kv_steps = {e: n for n, (kind, e) in enumerate(ORDER) if kind == "kv"}

    def project(n, _):
        pltpu.make_async_copy(wq_hbm.at[:, pl.ds(0, 256)], w_v.at[n], load_sem.at[n]).wait()
        pacc[...] = jnp.dot(tok_v[...], w_v[n], preferred_element_type=F32)

        def rows(e):
            cols = slice(e * DH, (e + 1) * DH)
            return pacc[0:rows_here, cols] + flag_cols * pacc[rows_here:rows_here + 1, cols]

        @pl.when(among(n, q_steps))
        def _():
            apart = n - q_steps[0]
            for e in range(2):
                i = (z // 2 + apart) % 2 * 2 + e
                m = apart * 2 + e
                stq[m] = turned_blocks((rope(rows(e)) * score_scale).astype(BF16))
                launch(*q_piece(m, i), i)

        @pl.when(jnp.logical_not(among(n, q_steps)))
        def _():
            high = among(n, (kv_steps[2], kv_steps[3])).astype(jnp.int32)
            low = among(n, (kv_steps[1], kv_steps[3])).astype(jnp.int32)
            i = (z // 2 + high) % 2 * 2 + (z + low) % 2
            m = 2 * high + low
            stkv[m, 0] = rope(rows(0)).astype(BF16)
            stkv[m, 1] = turned_blocks(rows(1).astype(BF16))
            launch(*kv_piece(high, low, i), i)
        return 0

    lax.fori_loop(0, 6, project, 0)

    acc[...] = jnp.zeros_like(acc)
    total_ref[...] = jnp.zeros_like(total_ref)
    sends = []

    def forward(slot, to_slot, s, h):
        def copy():
            return remote(kvb.at[slot], kvb.at[to_slot], f_send.at[n_send], kv_recv.at[to_slot], s, h)
        n_send = len(sends)
        sends.append(copy)
        copy().start()

    taken = set()

    def arrived(slot):
        if slot in taken:
            return
        taken.add(slot)
        remote(kvb.at[slot], kvb.at[slot], f_send.at[0], kv_recv.at[slot], seq, sib).wait_recv()
        if slot not in OWN_OF:
            return
        dx, d = OWN_OF[slot]
        if dx == 0:
            forward(slot, OWN[1, d], x_up, head)
            forward(slot, OWN[3, d], x_down, head)
        if dx == 1 and d in (0, 3):
            forward(slot, OWN[2, d], x_up, head)
        if dx == 3 and d in (1, 2):
            forward(slot, OWN[2, d], x_down, head)
        forward(slot, SIB[dx, d], seq, sib)

    for key in ((0, 0), (1, 0), (3, 0)):
        arrived(OWN[key])
    for j in range(4):
        remote(qb.at[j], qb.at[j], q_send.at[0], q_recv.at[j], seq, sib).wait_recv()
    q_dump = pltpu.make_async_copy(qb, q_out, dump_sem.at[16])
    q_dump.start()
    blocks = qb.shape[0]

    def step(t, _):
        for k in range(16):
            @pl.when(t == k)
            def _(k=k):
                for key in EARLY.get(k, ()):
                    arrived(OWN[key])
                arrived(2 * k)
                arrived(2 * k + 1)
                for action, n in EXTRA.get(k, ()):
                    if action == "own":
                        w_sib(16).start()
                    elif action == "in":
                        w_arrived(n)
                    else:
                        w_side(n)

        pltpu.make_async_copy(kvb.at[pl.ds(2 * t, 2)], kv_out.at[pl.ds(2 * t, 2)], dump_sem.at[t]).start()
        keys = kvb[pl.ds(2 * t, 2), 0].reshape(1024, DH)
        values = lanes(kvb[pl.ds(2 * t, 2), 1].reshape(8, DH, DH))

        def scores(i):
            return jnp.dot(keys, lanes(qb[i].reshape(4, DH, DH)), preferred_element_type=F32)

        now = scores(0)
        for i in range(blocks):
            later = scores(i + 1) if i + 1 < blocks else None
            cols = slice(i * 512, (i + 1) * 512)
            weights = jnp.exp2(now)
            total_ref[:, cols] += jnp.sum(weights.reshape(128, 8, 512), axis=0)
            acc[:, cols] += jnp.dot(values, weights.astype(BF16), preferred_element_type=F32)
            now = later
        return 0

    lax.fori_loop(0, 16, step, 0)

    for action, n in EXTRA[16]:
        w_arrived(n) if action == "in" else w_side(n)

    def finish(i, _):
        cols = pl.ds(pl.multiple_of(i * DH, DH), DH)
        total = jnp.sum(total_ref[:, cols], axis=0, keepdims=True)
        o_ref[cols, :] = (acc[:, cols] / total).astype(BF16).T
        return 0

    lax.fori_loop(0, blocks * 4, finish, 0)

    for n in range(17):
        w_sib(n).wait_recv()
        w_sib(n).wait_send()
    for n in range(len(CROSS)):
        w_cross(n).wait_send()
    for q in range(2):
        w_y(q).wait_send()
    for q in range(8):
        w_z(q).wait_send()
    for m in range(4):
        own = jnp.logical_and(straight, z % 2 == m) if m < 2 else None
        for there, alone in ((q_piece(m, 0)[0], own), (kv_piece(m // 2, m % 2, 0)[0], straight if m == 0 else None)):
            if alone is None:
                there.wait_send()
            else:
                pl.when(jnp.logical_not(alone))(there.wait_send)
    for copy in sends:
        copy().wait_send()
    q_dump.wait()

    def dumped(t, _):
        pltpu.make_async_copy(kvb.at[pl.ds(2 * t, 2)], kv_out.at[pl.ds(2 * t, 2)], dump_sem.at[t]).wait()
        return 0

    lax.fori_loop(0, 16, dumped, 0)


def repair_kernel(total_ref, q_hbm, kv_hbm, o_in, o_hbm, qb, kv, acc, peak, total, o_v, sem):
    sums = jnp.sum(total_ref[...], axis=0, keepdims=True)
    good = jnp.logical_and(sums > TOTAL_LOW, sums < TOTAL_HIGH)
    bad = jnp.max(jnp.where(good, 0.0, 1.0))

    @pl.when(bad > 0.5)
    def _():
        load = pltpu.make_async_copy(q_hbm, qb, sem)
        load.start()
        load.wait()
        acc[...] = jnp.zeros_like(acc)
        total[...] = jnp.zeros_like(total)
        peak[...] = jnp.full_like(peak, -3e38)

        def chunk(n, _):
            load = pltpu.make_async_copy(kv_hbm.at[n], kv, sem)
            load.start()
            load.wait()

            def block(i, _):
                cols = pl.ds(pl.multiple_of(i * 512, 512), 512)
                scores = jnp.dot(kv[0], lanes(qb[i].reshape(4, DH, DH)), preferred_element_type=F32)
                old = peak[0:1, cols]
                new = jnp.maximum(old, jnp.max(scores, axis=0, keepdims=True))
                factor = jnp.exp2(old - new)
                weights = jnp.exp2(scores - new)
                peak[0:1, cols] = new
                total[0:1, cols] = total[0:1, cols] * factor + jnp.sum(weights, axis=0, keepdims=True)
                acc[:, cols] = acc[:, cols] * factor + jnp.dot(
                    lanes(kv[1].reshape(4, DH, DH)), weights.astype(BF16), preferred_element_type=F32
                )
                return 0

            lax.fori_loop(0, 4, block, 0)
            return 0

        lax.fori_loop(0, kv_hbm.shape[0], chunk, 0)
        for n in range(16):
            cols = slice(n * DH, (n + 1) * DH)
            o_v[cols, :] = (acc[:, cols] / total[0:1, cols]).astype(BF16).T
        store = pltpu.make_async_copy(o_v, o_hbm, sem)
        store.start()
        store.wait()


def out_kernel(o_ref, wo_hbm, wg_hbm, out_ref, full, w_v, load_sem, send_sem, recv_sem):
    y_lo, x, z, y_hi, core = place()
    straight = core == y_lo
    groups = [(wo_hbm, y_hi * 2 + core), (wg_hbm.at[0], y_hi * 2 + 1 - core),
              (wg_hbm.at[1], (1 - y_hi) * 2 + core), (wg_hbm.at[2], (1 - y_hi) * 2 + 1 - core)]
    loads = [pltpu.make_async_copy(src, w_v.at[g], load_sem.at[n]) for n, (src, g) in enumerate(groups)]
    for load in loads:
        load.start()

    barrier = pltpu.get_barrier_semaphore()
    for hi in range(2):
        for lo in range(2):
            for zz in range(4):
                same = (straight, y_hi == hi, y_lo == lo, z == zz)

                @pl.when(jnp.logical_not(functools.reduce(jnp.logical_and, same)))
                def _(hi=hi, lo=lo, zz=zz):
                    pl.semaphore_signal(barrier, inc=1, device_id=(seq_of(lo, x, zz), hi * 2 + y_lo), device_id_type=MESH)

    @pl.when(straight)
    def _():
        pl.semaphore_wait(barrier, 15)

    @pl.when(jnp.logical_not(straight))
    def _():
        pl.semaphore_wait(barrier, 16)

    mine = y_hi * 8 + y_lo * 4 + z
    copies = []
    for dz in range(4):
        for hi in range(2):
            for c in range(2):
                zz = (z + dz) % 4
                n = (dz * 2 + hi) * 2 + c
                own = functools.reduce(jnp.logical_and, (straight, y_hi == hi, core == c, dz == 0)) if dz == 0 else None
                rows = pl.ds(pl.multiple_of(zz * 512 + hi * 256 + c * 128, 128), 128)
                far = remote(o_ref.at[rows], full.at[mine], send_sem.at[n], recv_sem.at[mine],
                             seq_of(core, x, zz), hi * 2 + c)
                near = pltpu.make_async_copy(o_ref.at[rows], full.at[mine], recv_sem.at[mine])
                copies.append((far, near, own))
    for far, near, own in copies:
        if own is None:
            far.start()
        else:
            pl.when(own)(near.start)
            pl.when(jnp.logical_not(own))(far.start)
    for load in loads:
        load.wait()
    for n in range(16):
        remote(full.at[n], full.at[n], send_sem.at[0], recv_sem.at[n], seq_of(y_lo, x, z), y_hi * 2 + 1 - core).wait_recv()
    attention = [lanes(full[4 * g:4 * g + 4]) for g in range(4)]

    def columns(n, _):
        cols = pl.ds(pl.multiple_of(n * 512, 512), 512)
        total = jnp.dot(attention[0], w_v[0, :, cols], preferred_element_type=F32)
        for g in range(1, 4):
            total += jnp.dot(attention[g], w_v[g, :, cols], preferred_element_type=F32)
        out_ref[:, cols] = total.astype(BF16)
        return 0

    lax.fori_loop(0, out_ref.shape[1] // 512, columns, 0)
    for far, near, own in copies:
        if own is None:
            far.wait_send()
        else:
            pl.when(jnp.logical_not(own))(far.wait_send)


def shards(tokens, mask_flags, mask_embed, w_query, w_key, w_value, w_out):
    rows, width = tokens.shape
    vmem, hbm = pl.BlockSpec(memory_space=pltpu.VMEM), pl.BlockSpec(memory_space=pl.ANY)
    dma = pltpu.SemaphoreType.DMA
    struct = jax.ShapeDtypeStruct
    attention, total, q_all, kv_all, w_all = pl.pallas_call(
        attend_kernel,
        out_shape=(
            struct((4 * rows, DH), BF16), struct((8, 4 * rows), F32), struct((4, rows, DH), BF16),
            struct((32, 2, rows, DH), BF16), struct((3,) + w_out.shape, BF16),
        ),
        in_specs=[hbm, vmem, vmem, hbm, hbm, hbm, hbm],
        out_specs=(vmem, vmem, hbm, hbm, hbm),
        scratch_shapes=[
            pltpu.VMEM((rows + 16, width), BF16),
            pltpu.VMEM((6, width, 256), BF16),
            pltpu.VMEM((rows + 16, 256), F32),
            pltpu.VMEM((rows, DH), F32),
            pltpu.VMEM((rows, DH), F32),
            pltpu.VMEM((4, rows, DH), BF16),
            pltpu.VMEM((4, 2, rows, DH), BF16),
            pltpu.VMEM((4, rows, DH), BF16),
            pltpu.VMEM((32, 2, rows, DH), BF16),
            pltpu.VMEM((DH, 4 * rows), F32),
            dma((7,)), dma((4,)), dma((4,)), dma((4,)), dma((32,)), dma((28,)), dma((17,)),
            dma((6,)), dma((2,)), dma((8,)), dma((8,)), dma((8,)), dma((17,)), dma((17,)),
        ],
        compiler_params=pltpu.CompilerParams(
            collective_id=0, has_side_effects=True, vmem_limit_bytes=VMEM_BYTES
        ),
        name="attend",
    )(tokens, mask_flags.reshape(1, rows), mask_embed, w_query, w_key, w_value, w_out)
    attention = pl.pallas_call(
        repair_kernel,
        out_shape=struct((4 * rows, DH), BF16),
        in_specs=[vmem, hbm, hbm, hbm],
        out_specs=hbm,
        scratch_shapes=[
            pltpu.VMEM((4, rows, DH), BF16),
            pltpu.VMEM((2, rows, DH), BF16),
            pltpu.VMEM((DH, 4 * rows), F32),
            pltpu.VMEM((8, 4 * rows), F32),
            pltpu.VMEM((8, 4 * rows), F32),
            pltpu.VMEM((4 * rows, DH), BF16),
            dma,
        ],
        input_output_aliases={3: 0},
        compiler_params=pltpu.CompilerParams(vmem_limit_bytes=VMEM_BYTES),
        name="repair",
    )(total, q_all, kv_all, attention)
    return pl.pallas_call(
        out_kernel,
        out_shape=struct((rows // 4, width), BF16),
        in_specs=[vmem, hbm, hbm],
        out_specs=vmem,
        scratch_shapes=[
            pltpu.VMEM((16, DH, DH), BF16),
            pltpu.VMEM((4,) + w_out.shape, BF16),
            dma((4,)), dma((16,)), dma((16,)),
        ],
        compiler_params=pltpu.CompilerParams(
            collective_id=1, has_side_effects=True, vmem_limit_bytes=VMEM_BYTES
        ),
        name="project_out",
    )(attention, w_out, w_all)


def solution(mesh):
    placed = (
        P("seq", None),
        P("seq"),
        P(),
        P(None, "head"),
        P(None, "head"),
        P(None, "head"),
        P("head", None),
    )
    return jax.shard_map(
        shards, mesh=mesh, in_specs=placed, out_specs=P(("seq", "head"), None), check_vma=False
    )
```

```python
import functools
import math

import jax
import jax.numpy as jnp
from jax import lax
from jax.experimental import pallas as pl
from jax.experimental.pallas import tpu as pltpu
from jax.sharding import PartitionSpec as P

DH = 128
MESH = pl.DeviceIdType.MESH
F32 = jnp.float32
BF16 = jnp.bfloat16
VMEM_BYTES = 60 * 2**20
TOTAL_LOW = 2.0**-60
TOTAL_HIGH = 2.0**100

USE = (
    ("own", 0, 0), ("sib", 0, 0), ("own", 1, 0), ("own", 3, 0), ("sib", 1, 0), ("sib", 3, 0), ("own", 2, 0), ("sib", 2, 0),
    ("own", 0, 1), ("sib", 0, 1), ("own", 1, 1), ("own", 3, 1), ("sib", 1, 1), ("sib", 3, 1), ("own", 0, 3), ("sib", 0, 3),
    ("own", 0, 2), ("sib", 0, 2), ("own", 1, 3), ("own", 3, 3), ("sib", 1, 3), ("sib", 3, 3), ("own", 2, 1), ("sib", 2, 1),
    ("own", 1, 2), ("own", 3, 2), ("sib", 1, 2), ("sib", 3, 2), ("own", 2, 3), ("sib", 2, 3), ("own", 2, 2), ("sib", 2, 2),
)
OWN = {(dx, e): n for n, (by, dx, e) in enumerate(USE) if by == "own"}
SIB = {(dx, e): n for n, (by, dx, e) in enumerate(USE) if by == "sib"}
EARLY = {2: ((2, 0), (0, 1)), 4: ((0, 3),), 7: ((0, 2),), 9: ((2, 1),), 13: ((2, 3),)}
OWN_OF = {slot: key for key, slot in OWN.items()}

ORDER = (("kv", 0), ("q", 0), ("q", 1), ("kv", 1), ("kv", 3), ("kv", 2))
LAST = 15
CROSS = (0, 1, 2, 3, 6, 7, 15)
EXTRA = {
    0: (("own", 0),), 4: (("in", 0),), 5: (("in", 1),), 6: (("in", 2), ("in", 3)), 8: (("in", 6),), 11: (("in", 7), ("side", 0)),
    12: (("in", 4), ("side", 1)), 13: (("in", 5), ("side", 2), ("side", 3)), 14: (("side", 6),),
    16: (("side", 7), ("side", 4), ("side", 5)),
}


def place():
    seq, head = lax.axis_index("seq"), lax.axis_index("head")
    y_lo, x, z = seq // 16, (seq // 4) % 4, seq % 4
    y_hi, core = head // 2, head % 2
    return y_lo, x, z, y_hi, core


def seq_of(y_lo, x, z):
    return y_lo * 16 + x * 4 + z


def remote(src, dst, send_sem, recv_sem, seq, head):
    return pltpu.make_async_remote_copy(
        src_ref=src, dst_ref=dst, send_sem=send_sem, recv_sem=recv_sem,
        device_id=(seq, head), device_id_type=MESH,
    )


def lanes(blocks):
    return jnp.concatenate([blocks[n] for n in range(blocks.shape[0])], axis=1)


def turned_blocks(rows):
    return jnp.concatenate(
        [rows[n * DH:(n + 1) * DH].T for n in range(rows.shape[0] // DH)], axis=0
    )


def attend_kernel(
    tok_hbm, flags_ref, embed_ref, wq_hbm, wk_hbm, wv_hbm, wo_hbm,
    out_ref, bad_ref,
    tok_v, w_v, pacc, cos_v, sin_v, stq, stkv, qb, kvb, acc, total_v, o_v, full, w_full, flag_v, out_acc,
    load_sem, q_send, q_recv, a_send, kv_recv, f_send,
    wx_send, wy_send, wx_recv, wz_send, wz_recv, ws_send, ws_recv, o_send, o_recv, flag_send, flag_recv,
):
    y_lo, x, z, y_hi, core = place()
    seq, head = seq_of(y_lo, x, z), y_hi * 2 + core
    sib = y_hi * 2 + (1 - core)
    straight = core == y_lo
    rows_here = tok_hbm.shape[0]
    x_up, x_down = seq_of(y_lo, (x + 1) % 4, z), seq_of(y_lo, (x + 3) % 4, z)
    z_up, z_down = seq_of(y_lo, x, (z + 1) % 4), seq_of(y_lo, x, (z + 3) % 4)
    y_seq = seq_of(1 - y_lo, x, z)
    cross_head = (1 - y_hi) * 2 + core

    def swapped(e):
        return 2 * ((z // 2 + e // 2) % 2) + (z % 2 + e % 2) % 2

    tok_load = pltpu.make_async_copy(tok_hbm, tok_v.at[pl.ds(0, rows_here)], load_sem.at[6])
    tok_load.start()
    for n, (kind, which) in enumerate(ORDER):
        if kind == "q":
            cols = pl.ds(pl.multiple_of(swapped(2 * which) // 2 * 256, 256), 256)
            pltpu.make_async_copy(wq_hbm.at[:, cols], w_v.at[n], load_sem.at[n]).start()
        else:
            cols = pl.ds(pl.multiple_of(swapped(which) * DH, DH), DH)
            pltpu.make_async_copy(wk_hbm.at[:, cols], w_v.at[n, :, pl.ds(0, DH)], load_sem.at[n]).start()
            pltpu.make_async_copy(wv_hbm.at[:, cols], w_v.at[n, :, pl.ds(DH, DH)], load_sem.at[n]).start()

    barrier = pltpu.get_barrier_semaphore()

    def greet(s, h):
        pl.semaphore_signal(barrier, inc=1, device_id=(s, h), device_id_type=MESH)

    for i in range(4):
        @pl.when(jnp.logical_not(jnp.logical_and(straight, z == i)))
        def _():
            greet(seq_of(core, x, i), y_hi * 2 + y_lo)
    for s, h in ((x_up, head), (x_down, head), (z_up, head), (z_down, head),
                 (seq, sib), (y_seq, head), (y_seq, cross_head)):
        greet(s, h)

    for hi in range(2):
        for lo in range(2):
            for zz in range(4):
                same = functools.reduce(jnp.logical_and, (straight, y_hi == hi, y_lo == lo, z == zz))

                @pl.when(jnp.logical_not(same))
                def _(hi=hi, lo=lo, zz=zz):
                    greet(seq_of(lo, x, zz), hi * 2 + y_lo)
    flag_peers = [(seq_of((y_lo + n // 4) % 2, x, (z + n) % 4), head) for n in range(1, 8)] + [
        (seq_of(y_lo, (x + n) % 4, z), head) for n in range(1, 4)
    ] + [(seq, (head + n) % 4) for n in range(1, 4)]
    for s, h in flag_peers:
        greet(s, h)

    lane = lax.broadcasted_iota(jnp.int32, (1, DH), 1)
    frequency = jnp.exp((lane % (DH // 2)).astype(F32) * (-2.0 * math.log(500000.0) / DH))
    sign = jnp.where(lane < DH // 2, -1.0, 1.0)

    def angle_rows(n, _):
        rows = pl.ds(pl.multiple_of(n * 64, 64), 64)
        position = (lax.broadcasted_iota(jnp.int32, (64, DH), 0) + (seq * rows_here + n * 64)).astype(F32)
        angle = position * frequency
        cos_v[rows, :] = jnp.cos(angle)
        sin_v[rows, :] = jnp.sin(angle) * sign
        return 0

    lax.fori_loop(0, rows_here // 64, angle_rows, 0)

    @pl.when(straight)
    def _():
        pl.semaphore_wait(barrier, 38)

    @pl.when(jnp.logical_not(straight))
    def _():
        pl.semaphore_wait(barrier, 40)

    def w_chunk(colour_y, colour_z, q):
        base = (colour_y * 2 + colour_z) * 128 + 32 * (q % 4)
        return pl.ds(pl.multiple_of(base, 32), 32)

    def w_rows(q, y=None, z_par=None):
        y = y_lo if y is None else y
        z_par = z % 2 if z_par is None else z_par
        return w_chunk(y if q < 4 else 1 - y, z_par, q)

    group = (1 - y_hi) * 2 + core

    def w_cross(n):
        q = CROSS[n]
        rows = w_rows(q, y=1 - y_lo) if q < 8 else w_rows(q - 8, y=1 - y_lo, z_par=1 - z % 2)
        return remote(wo_hbm.at[rows], w_full.at[head, rows], wx_send.at[n], wx_recv.at[CROSS[n]], y_seq, cross_head)

    def w_y(q):
        rows = w_rows(q)
        return remote(w_full.at[group, rows], w_full.at[group, rows], wy_send.at[q], wx_recv.at[q + 4], y_seq, head)

    def w_z(q, rows=None):
        rows = w_rows(q) if rows is None else rows
        return remote(w_full.at[group, rows], w_full.at[group, rows], wz_send.at[q], wz_recv.at[q],
                      z_up if q % 2 == 0 else z_down, head)

    def w_sib(n):
        if n == 16:
            return remote(wo_hbm, w_full.at[head], ws_send.at[16], ws_recv.at[16], seq, sib)
        rows = w_rows(n) if n < 8 else w_rows(n - 8, z_par=1 - z % 2)
        return remote(w_full.at[group, rows], w_full.at[group, rows], ws_send.at[n], ws_recv.at[n], seq, sib)

    def w_arrived(q):
        rows = w_rows(q)
        remote(w_full.at[group, rows], w_full.at[group, rows], wx_send.at[0], wx_recv.at[q], y_seq, head).wait_recv()
        if q < 2:
            w_y(q).start()
        if q + 8 not in CROSS:
            w_z(q).start()
        w_sib(q).start()

    def w_side(q):
        if q + 8 in CROSS:
            rows = w_rows(q, z_par=1 - z % 2)
            remote(w_full.at[group, rows], w_full.at[group, rows], wx_send.at[0], wx_recv.at[q + 8], y_seq, head).wait_recv()
            w_sib(8 + q).start()
            return
        w_z(q, w_rows(q, z_par=1 - z % 2)).wait_recv()
        w_sib(8 + q).start()

    for n in range(len(CROSS)):
        w_cross(n).start()
    own_w = pltpu.make_async_copy(wo_hbm, w_full.at[head], load_sem.at[7])

    flag_cols = jnp.broadcast_to(flags_ref[...].astype(F32), (DH, rows_here)).T
    width = tok_v.shape[1]
    tok_v[rows_here:, :] = jnp.broadcast_to(embed_ref[...].reshape(1, width), (16, width))
    tok_load.wait()

    def rope(rows):
        return rows * cos_v[...] + pltpu.roll(rows, DH // 2, 1) * sin_v[...]

    def q_piece(m, i):
        return (remote(stq.at[m], qb.at[z], q_send.at[m], q_recv.at[z], seq_of(core, x, i), y_hi * 2 + y_lo),
                pltpu.make_async_copy(stq.at[m], qb.at[z], q_recv.at[z]))

    def kv_piece(high, low, i):
        slot = (1 - high) * low * OWN[0, 1] + high * (OWN[0, 2] + low * (OWN[0, 3] - OWN[0, 2]))
        m = 2 * high + low
        return (remote(stkv.at[m], kvb.at[slot], a_send.at[m], kv_recv.at[slot],
                       seq_of(core, x, i), y_hi * 2 + y_lo),
                pltpu.make_async_copy(stkv.at[m], kvb.at[slot], kv_recv.at[slot]))

    def launch(there, here, i):
        own = jnp.logical_and(straight, z == i)
        pl.when(own)(here.start)
        pl.when(jnp.logical_not(own))(there.start)

    def among(n, picks):
        return functools.reduce(jnp.logical_or, [n == p for p in picks])

    sends = []

    def forward(slot, to_slot, s, h, only=None):
        def copy():
            return remote(kvb.at[slot], kvb.at[to_slot], f_send.at[n_send], kv_recv.at[to_slot], s, h)
        n_send = len(sends)
        sends.append((copy, only))
        if only is None:
            copy().start()
        else:
            pl.when(only)(copy().start)

    crooked = jnp.logical_not(straight)
    taken = set()

    def arrived(slot):
        if slot in taken:
            return
        taken.add(slot)
        remote(kvb.at[slot], kvb.at[slot], f_send.at[0], kv_recv.at[slot], seq, sib).wait_recv()
        if slot not in OWN_OF:
            return
        dx, d = OWN_OF[slot]
        if dx == 0:
            forward(slot, OWN[1, d], x_up, head)
            forward(slot, OWN[3, d], x_down, head)
        if dx == 1:
            forward(slot, OWN[2, d], x_up, head, straight if d in (0, 3) else crooked)
        if dx == 3:
            forward(slot, OWN[2, d], x_down, head, crooked if d in (0, 3) else straight)
        forward(slot, SIB[dx, d], seq, sib)

    score_scale = DH ** -0.5 * math.log2(math.e)
    q_steps = [n for n, (kind, _) in enumerate(ORDER) if kind == "q"]
    kv_steps = {e: n for n, (kind, e) in enumerate(ORDER) if kind == "kv"}

    def project(n, _):
        pltpu.make_async_copy(wq_hbm.at[:, pl.ds(0, 256)], w_v.at[n], load_sem.at[n]).wait()
        pacc[...] = jnp.dot(tok_v[...], w_v[n], preferred_element_type=F32)

        @pl.when(jnp.logical_or(jnp.logical_and(straight, n == 1), jnp.logical_and(crooked, n == 3)))
        def _():
            arrived(OWN[0, 0])

        def rows(e):
            cols = slice(e * DH, (e + 1) * DH)
            return pacc[0:rows_here, cols] + flag_cols * pacc[rows_here:rows_here + 1, cols]

        @pl.when(among(n, q_steps))
        def _():
            apart = n - q_steps[0]
            for e in range(2):
                i = (z // 2 + apart) % 2 * 2 + e
                m = apart * 2 + e
                stq[m] = turned_blocks((rope(rows(e)) * score_scale).astype(BF16))
                launch(*q_piece(m, i), i)

        @pl.when(jnp.logical_not(among(n, q_steps)))
        def _():
            high = among(n, (kv_steps[2], kv_steps[3])).astype(jnp.int32)
            low = among(n, (kv_steps[1], kv_steps[3])).astype(jnp.int32)
            i = (z // 2 + high) % 2 * 2 + (z + low) % 2
            m = 2 * high + low
            stkv[m, 0] = rope(rows(0)).astype(BF16)
            stkv[m, 1] = turned_blocks(rows(1).astype(BF16))

            @pl.when(high == 0)
            def _():
                launch(*kv_piece(high, low, i), i)
        return 0

    lax.fori_loop(0, 6, project, 0)

    acc[...] = jnp.zeros_like(acc)
    total_v[...] = jnp.zeros_like(total_v)
    for key in ((1, 0), (3, 0)):
        arrived(OWN[key])
    for j in range(4):
        remote(qb.at[j], qb.at[j], q_send.at[0], q_recv.at[j], seq, sib).wait_recv()
    own_w.start()
    kv_piece(1, 1, swapped(3))[0].start()
    blocks = qb.shape[0]

    def take(k):
        if k == 1:
            kv_piece(1, 0, swapped(2))[0].start()
        for key in EARLY.get(k, ()):
            arrived(OWN[key])
        arrived(2 * k)
        arrived(2 * k + 1)
        for action, n in EXTRA.get(k, ()):
            if action == "own":
                w_sib(16).start()
            elif action == "in":
                w_arrived(n)
            else:
                w_side(n)

    def chunk_pair(t):
        keys = kvb[pl.ds(2 * t, 2), 0].reshape(1024, DH)
        return keys, lanes(kvb[pl.ds(2 * t, 2), 1].reshape(8, DH, DH))

    def scores(keys, i):
        return jnp.dot(keys, lanes(qb[i].reshape(4, DH, DH)), preferred_element_type=F32)

    def add_weighted(now, values, cols):
        weights = jnp.exp2(now)
        total_v[:, cols] += jnp.sum(weights.reshape(128, 8, 512), axis=0)
        acc[:, cols] += jnp.dot(values, weights.astype(BF16), preferred_element_type=F32)

    def step(t, _):
        for k in range(LAST):
            pl.when(t == k)(functools.partial(take, k))
        keys, values = chunk_pair(t)
        now = scores(keys, 0)
        for i in range(blocks):
            later = scores(keys, i + 1) if i + 1 < blocks else None
            add_weighted(now, values, slice(i * 512, (i + 1) * 512))
            now = later
        return 0

    lax.fori_loop(0, LAST, step, 0)
    for k in range(LAST, 16):
        take(k)

    mine = y_hi * 8 + y_lo * 4 + z

    def o_piece(zz, hi, c):
        rows = pl.ds(pl.multiple_of(zz * 512 + hi * 256 + c * 128, 128), 128)
        return (remote(o_v.at[rows], full.at[mine], o_send.at[zz * 4 + hi * 2 + c], o_recv.at[mine],
                       seq_of(core, x, zz), hi * 2 + c),
                pltpu.make_async_copy(o_v.at[rows], full.at[mine], o_recv.at[mine]))

    def o_stays(zz, hi, c):
        return functools.reduce(jnp.logical_and, (straight, zz == z, y_hi == hi, core == c))

    def last(n, _):
        zz = (z + 1 + n) % 4
        cols = pl.ds(pl.multiple_of(zz * 512, 512), 512)
        pairs = [chunk_pair(t) for t in range(LAST, 16)]
        now = scores(pairs[0][0], zz)
        for k, (_, values) in enumerate(pairs):
            later = scores(pairs[k + 1][0], zz) if k + 1 < len(pairs) else None
            add_weighted(now, values, cols)
            now = later
        total = jnp.sum(total_v[:, cols], axis=0, keepdims=True)
        done = (acc[:, cols] / total).astype(BF16)
        for m in range(4):
            o_v[pl.ds(pl.multiple_of(zz * 512 + m * DH, DH), DH), :] = done[:, m * DH:(m + 1) * DH].T
        for hi in range(2):
            for c in range(2):
                there, here = o_piece(zz, hi, c)
                stays = o_stays(zz, hi, c)
                pl.when(stays)(here.start)
                pl.when(jnp.logical_not(stays))(there.start)
        return 0

    lax.fori_loop(0, blocks, last, 0)

    rounds = (range(0, 7), range(7, 10), range(10, 13))

    def flag(n):
        k = [n in r for r in rounds].index(True)
        return remote(flag_v.at[13 + k], flag_v.at[n], flag_send.at[n], flag_recv.at[n], *flag_peers[n])

    def tell(k):
        for n in rounds[k]:
            flag(n).start()

    def hear(k):
        for n in rounds[k]:
            flag(n).wait_recv()
        told = flag_v[13 + k]
        for n in rounds[k]:
            told = jnp.maximum(told, flag_v[n])
        return told

    sums = jnp.sum(total_v[...], axis=0, keepdims=True)
    good = jnp.logical_and(sums > TOTAL_LOW, sums < TOTAL_HIGH)
    flag_v[13] = jnp.broadcast_to(jnp.max(jnp.where(good, 0.0, 1.0), axis=1, keepdims=True), (8, DH))
    tell(0)
    for action, n in EXTRA[16]:
        w_arrived(n) if action == "in" else w_side(n)
    own_w.wait()
    for n in range(17):
        w_sib(n).wait_recv()

    def project_out(n, _):
        zz = (z + 3 - n) % 4
        for hi in range(4):
            remote(full.at[hi * 4 + zz], full.at[hi * 4 + zz], o_send.at[0], o_recv.at[hi * 4 + zz], seq, sib).wait_recv()
        attention = jnp.concatenate([full[hi * 4 + zz] for hi in range(4)], axis=1)
        depth = pl.ds(pl.multiple_of(zz * DH, DH), DH)

        def columns(m, _):
            cols = pl.ds(pl.multiple_of(m * 512, 512), 512)
            weights = jnp.concatenate([w_full[hi, depth, cols] for hi in range(4)], axis=0)
            out_acc[:, cols] += jnp.dot(attention, weights, preferred_element_type=F32)
            return 0

        lax.fori_loop(0, out_ref.shape[1] // 512, columns, 0)
        for k in range(2):
            @pl.when(n == k)
            def _(k=k):
                flag_v[14 + k] = hear(k)
                tell(k + 1)
        return 0

    out_acc[...] = jnp.zeros_like(out_acc)
    lax.fori_loop(0, 4, project_out, 0)
    out_ref[...] = out_acc[...].astype(BF16)
    bad_ref[0, 0] = jnp.max(hear(2))

    for n in range(13):
        flag(n).wait_send()
    for zz in range(4):
        for hi in range(2):
            for c in range(2):
                pl.when(jnp.logical_not(o_stays(zz, hi, c)))(o_piece(zz, hi, c)[0].wait_send)
    for n in range(17):
        w_sib(n).wait_send()
    for n in range(len(CROSS)):
        w_cross(n).wait_send()
    for q in range(2):
        w_y(q).wait_send()
    for q in range(8):
        if q + 8 not in CROSS:
            w_z(q).wait_send()
    for m in range(4):
        own = jnp.logical_and(straight, z % 2 == m) if m < 2 else None
        for there, alone in ((q_piece(m, 0)[0], own), (kv_piece(m // 2, m % 2, 0)[0], straight if m == 0 else None)):
            if alone is None:
                there.wait_send()
            else:
                pl.when(jnp.logical_not(alone))(there.wait_send)
    for copy, only in sends:
        if only is None:
            copy().wait_send()
        else:
            pl.when(only)(copy().wait_send)


def rotate(values, positions, head_size):
    halfway = head_size // 2
    indices = jnp.arange(halfway).astype(jnp.float32)
    frequency = jnp.exp(indices * (-2.0 * math.log(500000.0) / head_size))
    angles = positions[:, None] * frequency[None, :]
    cosine = jnp.cos(angles)[:, None, :]
    sine_table = jnp.sin(angles)[:, None, :]
    shaped = values.reshape(values.shape[0], -1, head_size)
    leading = shaped[..., :halfway]
    trailing = shaped[..., halfway:]
    turned = jnp.concatenate(
        [leading * cosine - trailing * sine_table, trailing * cosine + leading * sine_table],
        axis=-1,
    )
    return turned.reshape(values.shape)


def plain_shards(tokens, mask_flags, mask_embed, w_query, w_key, w_value, w_out):
    tok_rows = tokens.shape[0]
    head_size = DH
    heads_here = w_query.shape[1] // head_size
    mask_rows = mask_flags.astype(jnp.float32)[:, None]
    hidden = (
        tokens.astype(jnp.float32) + mask_rows * mask_embed.astype(jnp.float32)[None, :]
    ).astype(jnp.bfloat16)
    positions = (lax.axis_index("seq") * tok_rows + jnp.arange(tok_rows)).astype(jnp.float32)
    query_rows = rotate(
        jnp.dot(hidden, w_query, preferred_element_type=jnp.float32), positions, head_size
    ).astype(jnp.bfloat16)
    key_rows = rotate(
        jnp.dot(hidden, w_key, preferred_element_type=jnp.float32), positions, head_size
    ).astype(jnp.bfloat16)
    value_rows = jnp.dot(hidden, w_value, preferred_element_type=jnp.float32).astype(jnp.bfloat16)
    queries = query_rows.reshape(tok_rows, heads_here, head_size)
    score_scale = head_size ** (-0.5)
    row_peak = jnp.full((heads_here, tok_rows), -1e30, jnp.float32)
    weighted = jnp.zeros((tok_rows, heads_here, head_size), jnp.float32)
    peers = lax.axis_size("seq")
    ring = [(n, (n + 1) % peers) for n in range(peers)]

    def add_part(_, carried):
        keys, values, row_peak, total, weighted = carried
        scores = (
            jnp.einsum("qhd,khd->hqk", queries, keys.reshape(queries.shape), preferred_element_type=jnp.float32)
            * score_scale
        )
        new_peak = jnp.maximum(row_peak, jnp.max(scores, axis=-1))
        factor = jnp.exp(row_peak - new_peak)
        weights = jnp.exp(scores - new_peak[..., None])
        total = total * factor + jnp.sum(weights, axis=-1)
        update = jnp.einsum(
            "hqk,khd->qhd", weights.astype(jnp.bfloat16), values.reshape(queries.shape), preferred_element_type=jnp.float32
        )
        weighted = weighted * factor.T[:, :, None] + update
        return lax.ppermute(keys, "seq", ring), lax.ppermute(values, "seq", ring), new_peak, total, weighted

    _, _, _, total, weighted = lax.fori_loop(
        0, peers, add_part, (key_rows, value_rows, row_peak, jnp.zeros_like(row_peak), weighted)
    )
    attention = (weighted / total.T[:, :, None]).reshape(tok_rows, heads_here * head_size).astype(jnp.bfloat16)
    partials = jnp.dot(attention, w_out, preferred_element_type=jnp.float32)
    heads = lax.axis_size("head")
    here, part = lax.axis_index("head"), tok_rows // heads
    mixed_rows = lax.dynamic_slice_in_dim(partials, here * part, part, 0)
    for n in range(1, heads):
        leaving = lax.dynamic_slice_in_dim(partials, (here + n) % heads * part, part, 0)
        mixed_rows += lax.ppermute(leaving, "head", [(m, (m + n) % heads) for m in range(heads)])
    return mixed_rows.astype(jnp.bfloat16)


def shards(tokens, mask_flags, mask_embed, w_query, w_key, w_value, w_out):
    rows, width = tokens.shape
    vmem, hbm = pl.BlockSpec(memory_space=pltpu.VMEM), pl.BlockSpec(memory_space=pl.ANY)
    dma = pltpu.SemaphoreType.DMA
    struct = jax.ShapeDtypeStruct
    mixed_rows, bad = pl.pallas_call(
        attend_kernel,
        out_shape=(struct((rows // 4, width), BF16), struct((1, 1), F32)),
        in_specs=[hbm, vmem, vmem, hbm, hbm, hbm, hbm],
        out_specs=(vmem, pl.BlockSpec(memory_space=pltpu.SMEM)),
        scratch_shapes=[
            pltpu.VMEM((rows + 16, width), BF16),
            pltpu.VMEM((6, width, 256), BF16),
            pltpu.VMEM((rows + 16, 256), F32),
            pltpu.VMEM((rows, DH), F32),
            pltpu.VMEM((rows, DH), F32),
            pltpu.VMEM((4, rows, DH), BF16),
            pltpu.VMEM((4, 2, rows, DH), BF16),
            pltpu.VMEM((4, rows, DH), BF16),
            pltpu.VMEM((32, 2, rows, DH), BF16),
            pltpu.VMEM((DH, 4 * rows), F32),
            pltpu.VMEM((8, 4 * rows), F32),
            pltpu.VMEM((4 * rows, DH), BF16),
            pltpu.VMEM((16, DH, DH), BF16),
            pltpu.VMEM((4,) + w_out.shape, BF16),
            pltpu.VMEM((16, 8, DH), F32),
            pltpu.VMEM((rows // 4, width), F32),
            dma((8,)), dma((4,)), dma((4,)), dma((4,)), dma((32,)), dma((32,)),
            dma((7,)), dma((2,)), dma((16,)), dma((8,)), dma((8,)), dma((17,)), dma((17,)),
            dma((16,)), dma((16,)), dma((13,)), dma((13,)),
        ],
        compiler_params=pltpu.CompilerParams(
            collective_id=0, has_side_effects=True, vmem_limit_bytes=VMEM_BYTES
        ),
        name="attend",
    )(tokens, mask_flags.reshape(1, rows), mask_embed, w_query, w_key, w_value, w_out)
    return lax.cond(
        bad[0, 0] > 0.5,
        lambda: plain_shards(tokens, mask_flags, mask_embed, w_query, w_key, w_value, w_out),
        lambda: mixed_rows,
    )


def solution(mesh):
    placed = (
        P("seq", None),
        P("seq"),
        P(),
        P(None, "head"),
        P(None, "head"),
        P(None, "head"),
        P("head", None),
    )
    return jax.shard_map(
        shards, mesh=mesh, in_specs=placed, out_specs=P(("seq", "head"), None), check_vma=False
    )
```

```python
import functools
import math

import jax
import jax.numpy as jnp
from jax import lax
from jax.experimental import pallas as pl
from jax.experimental.pallas import tpu as pltpu
from jax.sharding import PartitionSpec as P

DH = 128
MESH = pl.DeviceIdType.MESH
F32 = jnp.float32
BF16 = jnp.bfloat16
VMEM_BYTES = 60 * 2**20
TOTAL_LOW = 2.0**-60
TOTAL_HIGH = 2.0**100

USE = (
    ("own", 0, 0), ("sib", 0, 0), ("own", 1, 0), ("own", 3, 0), ("sib", 1, 0), ("sib", 3, 0), ("own", 2, 0), ("sib", 2, 0),
    ("own", 0, 1), ("sib", 0, 1), ("own", 1, 1), ("own", 3, 1), ("sib", 1, 1), ("sib", 3, 1), ("own", 0, 3), ("sib", 0, 3),
    ("own", 0, 2), ("sib", 0, 2), ("own", 1, 3), ("own", 3, 3), ("sib", 1, 3), ("sib", 3, 3), ("own", 2, 1), ("sib", 2, 1),
    ("own", 1, 2), ("own", 3, 2), ("sib", 1, 2), ("sib", 3, 2), ("own", 2, 3), ("sib", 2, 3), ("own", 2, 2), ("sib", 2, 2),
)
OWN = {(dx, e): n for n, (by, dx, e) in enumerate(USE) if by == "own"}
SIB = {(dx, e): n for n, (by, dx, e) in enumerate(USE) if by == "sib"}
EARLY = {
    2: ((2, 0, None), (0, 1, None)), 4: ((0, 3, None),), 7: ((0, 2, None),), 9: ((2, 1, None),), 13: ((2, 3, None),),
}
OWN_OF = {slot: key for key, slot in OWN.items()}

ORDER = (("kv", 0), ("q", 0), ("q", 1), ("kv", 1), ("kv", 3), ("kv", 2))
LAST = 15
CROSS = (0, 1, 2, 3, 6, 7, 15)
EXTRA = {
    0: (("own", 0),), 4: (("in", 0),), 5: (("in", 1),), 6: (("in", 2), ("in", 3)), 8: (("in", 6),), 11: (("in", 7), ("side", 0)),
    12: (("in", 4), ("side", 1)), 13: (("in", 5), ("side", 2), ("side", 3)), 14: (("side", 6),),
    16: (("side", 7), ("side", 4), ("side", 5)),
}


def place():
    seq, head = lax.axis_index("seq"), lax.axis_index("head")
    y_lo, x, z = seq // 16, (seq // 4) % 4, seq % 4
    y_hi, core = head // 2, head % 2
    return y_lo, x, z, y_hi, core


def seq_of(y_lo, x, z):
    return y_lo * 16 + x * 4 + z


def block_order(n):
    return (2 + 3 * n + 3 * (n // 2) + 2 * (n // 3)) % 4


def remote(src, dst, send_sem, recv_sem, seq, head):
    return pltpu.make_async_remote_copy(
        src_ref=src, dst_ref=dst, send_sem=send_sem, recv_sem=recv_sem,
        device_id=(seq, head), device_id_type=MESH,
    )


def lanes(blocks):
    return jnp.concatenate([blocks[n] for n in range(blocks.shape[0])], axis=1)


def turned_blocks(rows):
    return jnp.concatenate(
        [rows[n * DH:(n + 1) * DH].T for n in range(rows.shape[0] // DH)], axis=0
    )


def attend_kernel(
    tok_hbm, flags_ref, embed_ref, wq_hbm, wk_hbm, wv_hbm, wo_hbm,
    out_ref, bad_ref,
    tok_v, w_v, pacc, cos_v, sin_v, stq, stkv, qb, kvb, acc, total_v, o_v, full, w_full, flag_v, out_acc,
    load_sem, q_send, q_recv, a_send, kv_recv, f_send,
    wx_send, wy_send, wx_recv, wz_send, wz_recv, ws_send, ws_recv, o_send, o_recv, flag_send, flag_recv,
):
    y_lo, x, z, y_hi, core = place()
    seq, head = seq_of(y_lo, x, z), y_hi * 2 + core
    sib = y_hi * 2 + (1 - core)
    straight = core == y_lo
    rows_here = tok_hbm.shape[0]
    x_up, x_down = seq_of(y_lo, (x + 1) % 4, z), seq_of(y_lo, (x + 3) % 4, z)
    z_up, z_down = seq_of(y_lo, x, (z + 1) % 4), seq_of(y_lo, x, (z + 3) % 4)
    y_seq = seq_of(1 - y_lo, x, z)
    cross_head = (1 - y_hi) * 2 + core

    def swapped(e):
        return 2 * ((z // 2 + e // 2) % 2) + (z % 2 + e % 2) % 2

    tok_load = pltpu.make_async_copy(tok_hbm, tok_v.at[pl.ds(0, rows_here)], load_sem.at[6])
    tok_load.start()
    for n, (kind, which) in enumerate(ORDER):
        if kind == "q":
            cols = pl.ds(pl.multiple_of(swapped(2 * which) // 2 * 256, 256), 256)
            pltpu.make_async_copy(wq_hbm.at[:, cols], w_v.at[n], load_sem.at[n]).start()
        else:
            cols = pl.ds(pl.multiple_of(swapped(which) * DH, DH), DH)
            pltpu.make_async_copy(wk_hbm.at[:, cols], w_v.at[n, :, pl.ds(0, DH)], load_sem.at[n]).start()
            pltpu.make_async_copy(wv_hbm.at[:, cols], w_v.at[n, :, pl.ds(DH, DH)], load_sem.at[n]).start()

    barrier = pltpu.get_barrier_semaphore()

    def greet(s, h):
        pl.semaphore_signal(barrier, inc=1, device_id=(s, h), device_id_type=MESH)

    for i in range(4):
        @pl.when(jnp.logical_not(jnp.logical_and(straight, z == i)))
        def _():
            greet(seq_of(core, x, i), y_hi * 2 + y_lo)
    for s, h in ((x_up, head), (x_down, head), (z_up, head), (z_down, head),
                 (seq, sib), (y_seq, head), (y_seq, cross_head)):
        greet(s, h)

    for hi in range(2):
        for lo in range(2):
            for zz in range(4):
                same = functools.reduce(jnp.logical_and, (straight, y_hi == hi, y_lo == lo, z == zz))

                @pl.when(jnp.logical_not(same))
                def _(hi=hi, lo=lo, zz=zz):
                    greet(seq_of(lo, x, zz), hi * 2 + y_lo)
    flag_peers = [(seq_of((y_lo + n // 4) % 2, x, (z + n) % 4), head) for n in range(1, 8)] + [
        (seq_of(y_lo, (x + n) % 4, z), head) for n in range(1, 4)
    ] + [(seq, (head + n) % 4) for n in range(1, 4)]
    for s, h in flag_peers:
        greet(s, h)

    lane = lax.broadcasted_iota(jnp.int32, (1, DH), 1)
    frequency = jnp.exp((lane % (DH // 2)).astype(F32) * (-2.0 * math.log(500000.0) / DH))
    sign = jnp.where(lane < DH // 2, -1.0, 1.0)

    def angle_rows(n, _):
        rows = pl.ds(pl.multiple_of(n * 64, 64), 64)
        position = (lax.broadcasted_iota(jnp.int32, (64, DH), 0) + (seq * rows_here + n * 64)).astype(F32)
        angle = position * frequency
        cos_v[rows, :] = jnp.cos(angle)
        sin_v[rows, :] = jnp.sin(angle) * sign
        return 0

    lax.fori_loop(0, rows_here // 64, angle_rows, 0)

    def w_chunk(colour_y, colour_z, q):
        base = (colour_y * 2 + colour_z) * 128 + 32 * (q % 4)
        return pl.ds(pl.multiple_of(base, 32), 32)

    def w_rows(q, y=None, z_par=None):
        y = y_lo if y is None else y
        z_par = z % 2 if z_par is None else z_par
        return w_chunk(y if q < 4 else 1 - y, z_par, q)

    group = (1 - y_hi) * 2 + core

    def w_cross(n):
        q = CROSS[n]
        rows = w_rows(q, y=1 - y_lo) if q < 8 else w_rows(q - 8, y=1 - y_lo, z_par=1 - z % 2)
        return remote(wo_hbm.at[rows], w_full.at[head, rows], wx_send.at[n], wx_recv.at[CROSS[n]], y_seq, cross_head)

    def w_y(q):
        rows = w_rows(q)
        return remote(w_full.at[group, rows], w_full.at[group, rows], wy_send.at[q], wx_recv.at[q + 4], y_seq, head)

    def w_z(q, rows=None):
        rows = w_rows(q) if rows is None else rows
        return remote(w_full.at[group, rows], w_full.at[group, rows], wz_send.at[q], wz_recv.at[q],
                      z_up if q % 2 == 0 else z_down, head)

    def w_sib(n):
        if n == 16:
            return remote(wo_hbm, w_full.at[head], ws_send.at[16], ws_recv.at[16], seq, sib)
        rows = w_rows(n) if n < 8 else w_rows(n - 8, z_par=1 - z % 2)
        return remote(w_full.at[group, rows], w_full.at[group, rows], ws_send.at[n], ws_recv.at[n], seq, sib)

    def w_arrived(q):
        rows = w_rows(q)
        remote(w_full.at[group, rows], w_full.at[group, rows], wx_send.at[0], wx_recv.at[q], y_seq, head).wait_recv()
        if q < 2:
            w_y(q).start()
        if q + 8 not in CROSS:
            w_z(q).start()
        w_sib(q).start()

    def w_side(q):
        if q + 8 in CROSS:
            rows = w_rows(q, z_par=1 - z % 2)
            remote(w_full.at[group, rows], w_full.at[group, rows], wx_send.at[0], wx_recv.at[q + 8], y_seq, head).wait_recv()
            w_sib(8 + q).start()
            return
        w_z(q, w_rows(q, z_par=1 - z % 2)).wait_recv()
        w_sib(8 + q).start()

    own_w = pltpu.make_async_copy(wo_hbm, w_full.at[head], load_sem.at[7])

    flag_cols = jnp.broadcast_to(flags_ref[...].astype(F32), (DH, rows_here)).T
    width = tok_v.shape[1]
    tok_v[rows_here:, :] = jnp.broadcast_to(embed_ref[...].reshape(1, width), (16, width))
    tok_load.wait()

    def rope(rows):
        return rows * cos_v[...] + pltpu.roll(rows, DH // 2, 1) * sin_v[...]

    def q_piece(m, i):
        return (remote(stq.at[m], qb.at[z], q_send.at[m], q_recv.at[z], seq_of(core, x, i), y_hi * 2 + y_lo),
                pltpu.make_async_copy(stq.at[m], qb.at[z], q_recv.at[z]))

    def kv_piece(high, low, i):
        slot = (1 - high) * low * OWN[0, 1] + high * (OWN[0, 2] + low * (OWN[0, 3] - OWN[0, 2]))
        m = 2 * high + low
        return (remote(stkv.at[m], kvb.at[slot], a_send.at[m], kv_recv.at[slot],
                       seq_of(core, x, i), y_hi * 2 + y_lo),
                pltpu.make_async_copy(stkv.at[m], kvb.at[slot], kv_recv.at[slot]))

    def launch(there, here, i):
        own = jnp.logical_and(straight, z == i)
        pl.when(own)(here.start)
        pl.when(jnp.logical_not(own))(there.start)

    def among(n, picks):
        return functools.reduce(jnp.logical_or, [n == p for p in picks])

    crooked = jnp.logical_not(straight)
    sends = {}

    def forward(slot, to_slot, s, h, only=None):
        n_send = sends.setdefault((slot, to_slot), (len(sends), s, h, only))[0]
        copy = remote(kvb.at[slot], kvb.at[to_slot], f_send.at[n_send], kv_recv.at[to_slot], s, h)
        if only is None:
            copy.start()
        else:
            pl.when(only)(copy.start)

    def take_up(slot):
        remote(kvb.at[slot], kvb.at[slot], f_send.at[0], kv_recv.at[slot], seq, sib).wait_recv()
        if slot not in OWN_OF:
            return
        dx, d = OWN_OF[slot]
        if dx == 0:
            forward(slot, OWN[1, d], x_up, head)
            forward(slot, OWN[3, d], x_down, head)
        if dx == 1:
            forward(slot, OWN[2, d], x_up, head, straight if d in (0, 3) else crooked)
        if dx == 3:
            forward(slot, OWN[2, d], x_down, head, crooked if d in (0, 3) else straight)
        forward(slot, SIB[dx, d], seq, sib)

    taken = set()

    def arrived(slot, kind=None):
        if slot in taken:
            return
        if kind is None:
            taken.add(slot)
            take_up(slot)
        else:
            if kind == "crooked":
                taken.add(slot)
            pl.when(straight if kind == "straight" else crooked)(functools.partial(take_up, slot))

    score_scale = DH ** -0.5 * math.log2(math.e)
    q_steps = [n for n, (kind, _) in enumerate(ORDER) if kind == "q"]
    kv_steps = {e: n for n, (kind, e) in enumerate(ORDER) if kind == "kv"}

    def project(n, _):
        pltpu.make_async_copy(wq_hbm.at[:, pl.ds(0, 256)], w_v.at[n], load_sem.at[n]).wait()
        pacc[...] = jnp.dot(tok_v[...], w_v[n], preferred_element_type=F32)

        @pl.when(n == 0)
        def _():
            @pl.when(straight)
            def _():
                pl.semaphore_wait(barrier, 38)

            @pl.when(jnp.logical_not(straight))
            def _():
                pl.semaphore_wait(barrier, 40)

            for k in range(len(CROSS)):
                w_cross(k).start()

        @pl.when(jnp.logical_or(jnp.logical_and(straight, n == 1), jnp.logical_and(crooked, n == 3)))
        def _():
            taken.add(OWN[0, 0])
            take_up(OWN[0, 0])

        def rows(e):
            cols = slice(e * DH, (e + 1) * DH)
            return pacc[0:rows_here, cols] + flag_cols * pacc[rows_here:rows_here + 1, cols]

        @pl.when(among(n, q_steps))
        def _():
            apart = n - q_steps[0]
            for e in range(2):
                i = (z // 2 + apart) % 2 * 2 + e
                m = apart * 2 + e
                stq[m] = turned_blocks((rope(rows(e)) * score_scale).astype(BF16))
                launch(*q_piece(m, i), i)

        @pl.when(jnp.logical_not(among(n, q_steps)))
        def _():
            high = among(n, (kv_steps[2], kv_steps[3])).astype(jnp.int32)
            low = among(n, (kv_steps[1], kv_steps[3])).astype(jnp.int32)
            i = (z // 2 + high) % 2 * 2 + (z + low) % 2
            m = 2 * high + low
            stkv[m, 0] = rope(rows(0)).astype(BF16)
            stkv[m, 1] = turned_blocks(rows(1).astype(BF16))

            @pl.when(jnp.logical_or(high == 0, straight))
            def _():
                launch(*kv_piece(high, low, i), i)
        return 0

    lax.fori_loop(0, 6, project, 0)

    acc[...] = jnp.zeros_like(acc)
    total_v[...] = jnp.zeros_like(total_v)
    for key in ((1, 0), (3, 0)):
        arrived(OWN[key])
    for j in range(4):
        remote(qb.at[j], qb.at[j], q_send.at[0], q_recv.at[j], seq, sib).wait_recv()
    own_w.start()
    pl.when(crooked)(kv_piece(1, 1, swapped(3))[0].start)
    blocks = qb.shape[0]

    def take(k):
        if k == 1:
            pl.when(crooked)(kv_piece(1, 0, swapped(2))[0].start)
        for dx, e, kind in EARLY.get(k, ()):
            arrived(OWN[dx, e], kind)
        arrived(2 * k)
        arrived(2 * k + 1)
        for action, n in EXTRA.get(k, ()):
            if action == "own":
                w_sib(16).start()
            elif action == "in":
                w_arrived(n)
            else:
                w_side(n)

    def chunk_pair(t):
        keys = kvb[pl.ds(2 * t, 2), 0].reshape(1024, DH)
        return keys, lanes(kvb[pl.ds(2 * t, 2), 1].reshape(8, DH, DH))

    def scores(keys, i):
        return jnp.dot(keys, lanes(qb[i].reshape(4, DH, DH)), preferred_element_type=F32)

    def add_weighted(now, values, cols):
        weights = jnp.exp2(now)
        total_v[:, cols] += jnp.sum(weights.reshape(128, 8, 512), axis=0)
        acc[:, cols] += jnp.dot(values, weights.astype(BF16), preferred_element_type=F32)

    def step(t, _):
        for k in range(LAST):
            pl.when(t == k)(functools.partial(take, k))
        keys, values = chunk_pair(t)
        now = scores(keys, 0)
        for i in range(blocks):
            later = scores(keys, i + 1) if i + 1 < blocks else None
            add_weighted(now, values, slice(i * 512, (i + 1) * 512))
            now = later
        return 0

    lax.fori_loop(0, LAST, step, 0)
    for k in range(LAST, 16):
        take(k)

    mine = y_hi * 8 + y_lo * 4 + z

    def o_piece(zz, hi, c):
        rows = pl.ds(pl.multiple_of(zz * 512 + hi * 256 + c * 128, 128), 128)
        return (remote(o_v.at[rows], full.at[mine], o_send.at[zz * 4 + hi * 2 + c], o_recv.at[mine],
                       seq_of(core, x, zz), hi * 2 + c),
                pltpu.make_async_copy(o_v.at[rows], full.at[mine], o_recv.at[mine]))

    def o_stays(zz, hi, c):
        return functools.reduce(jnp.logical_and, (straight, zz == z, y_hi == hi, core == c))

    def last(n, _):
        zz = (z + block_order(n)) % 4
        cols = pl.ds(pl.multiple_of(zz * 512, 512), 512)
        pairs = [chunk_pair(t) for t in range(LAST, 16)]
        now = scores(pairs[0][0], zz)
        for k, (_, values) in enumerate(pairs):
            later = scores(pairs[k + 1][0], zz) if k + 1 < len(pairs) else None
            add_weighted(now, values, cols)
            now = later
        total = jnp.sum(total_v[:, cols], axis=0, keepdims=True)
        done = (acc[:, cols] / total).astype(BF16)
        for m in range(4):
            o_v[pl.ds(pl.multiple_of(zz * 512 + m * DH, DH), DH), :] = done[:, m * DH:(m + 1) * DH].T
        for hi in range(2):
            for c in range(2):
                there, here = o_piece(zz, hi, c)
                stays = o_stays(zz, hi, c)
                pl.when(stays)(here.start)
                pl.when(jnp.logical_not(stays))(there.start)
        return 0

    lax.fori_loop(0, blocks, last, 0)

    rounds = (range(0, 7), range(7, 10), range(10, 13))

    def flag(n):
        k = [n in r for r in rounds].index(True)
        return remote(flag_v.at[13 + k], flag_v.at[n], flag_send.at[n], flag_recv.at[n], *flag_peers[n])

    def tell(k):
        for n in rounds[k]:
            flag(n).start()

    def hear(k):
        for n in rounds[k]:
            flag(n).wait_recv()
        told = flag_v[13 + k]
        for n in rounds[k]:
            told = jnp.maximum(told, flag_v[n])
        return told

    sums = jnp.sum(total_v[...], axis=0, keepdims=True)
    good = jnp.logical_and(sums > TOTAL_LOW, sums < TOTAL_HIGH)
    flag_v[13] = jnp.broadcast_to(jnp.max(jnp.where(good, 0.0, 1.0), axis=1, keepdims=True), (8, DH))
    tell(0)
    for action, n in EXTRA[16]:
        w_arrived(n) if action == "in" else w_side(n)
    own_w.wait()
    for n in range(17):
        w_sib(n).wait_recv()

    def project_out(n, _):
        zz = (z + 4 - block_order(n)) % 4
        for hi in range(4):
            remote(full.at[hi * 4 + zz], full.at[hi * 4 + zz], o_send.at[0], o_recv.at[hi * 4 + zz], seq, sib).wait_recv()
        attention = jnp.concatenate([full[hi * 4 + zz] for hi in range(4)], axis=1)
        depth = pl.ds(pl.multiple_of(zz * DH, DH), DH)

        def columns(m, _):
            cols = pl.ds(pl.multiple_of(m * 512, 512), 512)
            weights = jnp.concatenate([w_full[hi, depth, cols] for hi in range(4)], axis=0)
            out_acc[:, cols] += jnp.dot(attention, weights, preferred_element_type=F32)
            return 0

        lax.fori_loop(0, out_ref.shape[1] // 512, columns, 0)
        for k in range(2):
            @pl.when(n == k)
            def _(k=k):
                flag_v[14 + k] = hear(k)
                tell(k + 1)
        return 0

    out_acc[...] = jnp.zeros_like(out_acc)
    lax.fori_loop(0, 4, project_out, 0)
    out_ref[...] = out_acc[...].astype(BF16)
    bad_ref[0, 0] = jnp.max(hear(2))

    for n in range(13):
        flag(n).wait_send()
    for zz in range(4):
        for hi in range(2):
            for c in range(2):
                pl.when(jnp.logical_not(o_stays(zz, hi, c)))(o_piece(zz, hi, c)[0].wait_send)
    for n in range(17):
        w_sib(n).wait_send()
    for n in range(len(CROSS)):
        w_cross(n).wait_send()
    for q in range(2):
        w_y(q).wait_send()
    for q in range(8):
        if q + 8 not in CROSS:
            w_z(q).wait_send()
    for m in range(4):
        own = jnp.logical_and(straight, z % 2 == m) if m < 2 else None
        for there, alone in ((q_piece(m, 0)[0], own), (kv_piece(m // 2, m % 2, 0)[0], straight if m == 0 else None)):
            if alone is None:
                there.wait_send()
            else:
                pl.when(jnp.logical_not(alone))(there.wait_send)
    for (slot, to_slot), (n, s, h, only) in sends.items():
        copy = remote(kvb.at[slot], kvb.at[to_slot], f_send.at[n], kv_recv.at[to_slot], s, h)
        if only is None:
            copy.wait_send()
        else:
            pl.when(only)(copy.wait_send)


def rotate(values, positions, head_size):
    halfway = head_size // 2
    indices = jnp.arange(halfway).astype(jnp.float32)
    frequency = jnp.exp(indices * (-2.0 * math.log(500000.0) / head_size))
    angles = positions[:, None] * frequency[None, :]
    cosine = jnp.cos(angles)[:, None, :]
    sine_table = jnp.sin(angles)[:, None, :]
    shaped = values.reshape(values.shape[0], -1, head_size)
    leading = shaped[..., :halfway]
    trailing = shaped[..., halfway:]
    turned = jnp.concatenate(
        [leading * cosine - trailing * sine_table, trailing * cosine + leading * sine_table],
        axis=-1,
    )
    return turned.reshape(values.shape)


def plain_shards(tokens, mask_flags, mask_embed, w_query, w_key, w_value, w_out):
    tok_rows = tokens.shape[0]
    head_size = DH
    heads_here = w_query.shape[1] // head_size
    mask_rows = mask_flags.astype(jnp.float32)[:, None]
    hidden = (
        tokens.astype(jnp.float32) + mask_rows * mask_embed.astype(jnp.float32)[None, :]
    ).astype(jnp.bfloat16)
    positions = (lax.axis_index("seq") * tok_rows + jnp.arange(tok_rows)).astype(jnp.float32)
    query_rows = rotate(
        jnp.dot(hidden, w_query, preferred_element_type=jnp.float32), positions, head_size
    ).astype(jnp.bfloat16)
    key_rows = rotate(
        jnp.dot(hidden, w_key, preferred_element_type=jnp.float32), positions, head_size
    ).astype(jnp.bfloat16)
    value_rows = jnp.dot(hidden, w_value, preferred_element_type=jnp.float32).astype(jnp.bfloat16)
    queries = query_rows.reshape(tok_rows, heads_here, head_size)
    score_scale = head_size ** (-0.5)
    row_peak = jnp.full((heads_here, tok_rows), -1e30, jnp.float32)
    weighted = jnp.zeros((tok_rows, heads_here, head_size), jnp.float32)
    peers = lax.axis_size("seq")
    ring = [(n, (n + 1) % peers) for n in range(peers)]

    def add_part(_, carried):
        keys, values, row_peak, total, weighted = carried
        scores = (
            jnp.einsum("qhd,khd->hqk", queries, keys.reshape(queries.shape), preferred_element_type=jnp.float32)
            * score_scale
        )
        new_peak = jnp.maximum(row_peak, jnp.max(scores, axis=-1))
        factor = jnp.exp(row_peak - new_peak)
        weights = jnp.exp(scores - new_peak[..., None])
        total = total * factor + jnp.sum(weights, axis=-1)
        update = jnp.einsum(
            "hqk,khd->qhd", weights.astype(jnp.bfloat16), values.reshape(queries.shape), preferred_element_type=jnp.float32
        )
        weighted = weighted * factor.T[:, :, None] + update
        return lax.ppermute(keys, "seq", ring), lax.ppermute(values, "seq", ring), new_peak, total, weighted

    _, _, _, total, weighted = lax.fori_loop(
        0, peers, add_part, (key_rows, value_rows, row_peak, jnp.zeros_like(row_peak), weighted)
    )
    attention = (weighted / total.T[:, :, None]).reshape(tok_rows, heads_here * head_size).astype(jnp.bfloat16)
    partials = jnp.dot(attention, w_out, preferred_element_type=jnp.float32)
    heads = lax.axis_size("head")
    here, part = lax.axis_index("head"), tok_rows // heads
    mixed_rows = lax.dynamic_slice_in_dim(partials, here * part, part, 0)
    for n in range(1, heads):
        leaving = lax.dynamic_slice_in_dim(partials, (here + n) % heads * part, part, 0)
        mixed_rows += lax.ppermute(leaving, "head", [(m, (m + n) % heads) for m in range(heads)])
    return mixed_rows.astype(jnp.bfloat16)


def shards(tokens, mask_flags, mask_embed, w_query, w_key, w_value, w_out):
    rows, width = tokens.shape
    vmem, hbm = pl.BlockSpec(memory_space=pltpu.VMEM), pl.BlockSpec(memory_space=pl.ANY)
    dma = pltpu.SemaphoreType.DMA
    struct = jax.ShapeDtypeStruct
    mixed_rows, bad = pl.pallas_call(
        attend_kernel,
        out_shape=(struct((rows // 4, width), BF16), struct((1, 1), F32)),
        in_specs=[hbm, vmem, vmem, hbm, hbm, hbm, hbm],
        out_specs=(vmem, pl.BlockSpec(memory_space=pltpu.SMEM)),
        scratch_shapes=[
            pltpu.VMEM((rows + 16, width), BF16),
            pltpu.VMEM((6, width, 256), BF16),
            pltpu.VMEM((rows + 16, 256), F32),
            pltpu.VMEM((rows, DH), F32),
            pltpu.VMEM((rows, DH), F32),
            pltpu.VMEM((4, rows, DH), BF16),
            pltpu.VMEM((4, 2, rows, DH), BF16),
            pltpu.VMEM((4, rows, DH), BF16),
            pltpu.VMEM((32, 2, rows, DH), BF16),
            pltpu.VMEM((DH, 4 * rows), F32),
            pltpu.VMEM((8, 4 * rows), F32),
            pltpu.VMEM((4 * rows, DH), BF16),
            pltpu.VMEM((16, DH, DH), BF16),
            pltpu.VMEM((4,) + w_out.shape, BF16),
            pltpu.VMEM((16, 8, DH), F32),
            pltpu.VMEM((rows // 4, width), F32),
            dma((8,)), dma((4,)), dma((4,)), dma((4,)), dma((32,)), dma((32,)),
            dma((7,)), dma((2,)), dma((16,)), dma((8,)), dma((8,)), dma((17,)), dma((17,)),
            dma((16,)), dma((16,)), dma((13,)), dma((13,)),
        ],
        compiler_params=pltpu.CompilerParams(
            collective_id=0, has_side_effects=True, vmem_limit_bytes=VMEM_BYTES
        ),
        name="attend",
    )(tokens, mask_flags.reshape(1, rows), mask_embed, w_query, w_key, w_value, w_out)
    return lax.cond(
        bad[0, 0] > 0.5,
        lambda: plain_shards(tokens, mask_flags, mask_embed, w_query, w_key, w_value, w_out),
        lambda: mixed_rows,
    )


def solution(mesh):
    placed = (
        P("seq", None),
        P("seq"),
        P(),
        P(None, "head"),
        P(None, "head"),
        P(None, "head"),
        P("head", None),
    )
    return jax.shard_map(
        shards, mesh=mesh, in_specs=placed, out_specs=P(("seq", "head"), None), check_vma=False
    )
```

```python
import functools
import math

import jax
import jax.numpy as jnp
from jax import lax
from jax.experimental import pallas as pl
from jax.experimental.pallas import tpu as pltpu
from jax.sharding import PartitionSpec as P

DH = 128
MESH = pl.DeviceIdType.MESH
F32 = jnp.float32
BF16 = jnp.bfloat16
VMEM_BYTES = 60 * 2**20
TOTAL_LOW = 2.0**-60
TOTAL_HIGH = 2.0**100

USE = (
    ("own", 0, 0), ("sib", 0, 0), ("own", 1, 0), ("own", 3, 0), ("sib", 1, 0), ("sib", 3, 0), ("own", 2, 0), ("sib", 2, 0),
    ("own", 0, 1), ("sib", 0, 1), ("own", 1, 1), ("own", 3, 1), ("sib", 1, 1), ("sib", 3, 1), ("own", 0, 3), ("sib", 0, 3),
    ("own", 0, 2), ("sib", 0, 2), ("own", 1, 3), ("own", 3, 3), ("sib", 1, 3), ("sib", 3, 3), ("own", 2, 1), ("sib", 2, 1),
    ("own", 1, 2), ("own", 3, 2), ("sib", 1, 2), ("sib", 3, 2), ("own", 2, 3), ("sib", 2, 3), ("own", 2, 2), ("sib", 2, 2),
)
OWN = {(dx, e): n for n, (by, dx, e) in enumerate(USE) if by == "own"}
SIB = {(dx, e): n for n, (by, dx, e) in enumerate(USE) if by == "sib"}
EARLY = {
    2: ((2, 0, None), (0, 1, None)), 4: ((0, 3, None),), 7: ((0, 2, None),), 9: ((2, 1, None),), 13: ((2, 3, None),),
}
OWN_OF = {slot: key for key, slot in OWN.items()}

ORDER = (("kv", 0), ("q", 0), ("q", 1), ("kv", 1), ("kv", 3), ("kv", 2))
LAST = 15
CROSS = (0, 1, 2, 3, 6, 7, 15)
EXTRA = {
    0: (("own", 0),), 2: (("in", 0),), 3: (("in", 1),), 5: (("in", 2),), 7: (("in", 3),), 9: (("in", 6),), 10: (("side", 0), ("side", 1)),
    11: (("in", 7), ("in", 4)), 12: (("in", 5), ("side", 2)), 13: (("side", 3),), 14: (("side", 6),),
    16: (("side", 7), ("side", 4), ("side", 5)),
}


def place():
    seq, head = lax.axis_index("seq"), lax.axis_index("head")
    y_lo, x, z = seq // 16, (seq // 4) % 4, seq % 4
    y_hi, core = head // 2, head % 2
    return y_lo, x, z, y_hi, core


def seq_of(y_lo, x, z):
    return y_lo * 16 + x * 4 + z


def block_order(n):
    return (2 + 3 * n + 3 * (n // 2) + 2 * (n // 3)) % 4


def remote(src, dst, send_sem, recv_sem, seq, head):
    return pltpu.make_async_remote_copy(
        src_ref=src, dst_ref=dst, send_sem=send_sem, recv_sem=recv_sem,
        device_id=(seq, head), device_id_type=MESH,
    )


def lanes(blocks):
    return jnp.concatenate([blocks[n] for n in range(blocks.shape[0])], axis=1)


def turned_blocks(rows):
    return jnp.concatenate(
        [rows[n * DH:(n + 1) * DH].T for n in range(rows.shape[0] // DH)], axis=0
    )


def attend_kernel(
    tok_hbm, flags_ref, embed_ref, wq_hbm, wk_hbm, wv_hbm, wo_hbm,
    out_ref, bad_ref,
    tok_v, w_v, pacc, cos_v, sin_v, stq, stkv, qb, kvb, acc, total_v, o_v, full, w_full, flag_v, out_acc,
    load_sem, q_send, q_recv, a_send, kv_recv, f_send,
    wx_send, wy_send, wx_recv, wz_send, wz_recv, ws_send, ws_recv, o_send, o_recv, flag_send, flag_recv,
):
    y_lo, x, z, y_hi, core = place()
    seq, head = seq_of(y_lo, x, z), y_hi * 2 + core
    sib = y_hi * 2 + (1 - core)
    straight = core == y_lo
    rows_here = tok_hbm.shape[0]
    x_up, x_down = seq_of(y_lo, (x + 1) % 4, z), seq_of(y_lo, (x + 3) % 4, z)
    z_up, z_down = seq_of(y_lo, x, (z + 1) % 4), seq_of(y_lo, x, (z + 3) % 4)
    y_seq = seq_of(1 - y_lo, x, z)
    cross_head = (1 - y_hi) * 2 + core

    def swapped(e):
        return 2 * ((z // 2 + e // 2) % 2) + (z % 2 + e % 2) % 2

    tok_load = pltpu.make_async_copy(tok_hbm, tok_v.at[pl.ds(0, rows_here)], load_sem.at[6])
    tok_load.start()
    for n, (kind, which) in enumerate(ORDER):
        if kind == "q":
            cols = pl.ds(pl.multiple_of(swapped(2 * which) // 2 * 256, 256), 256)
            pltpu.make_async_copy(wq_hbm.at[:, cols], w_v.at[n], load_sem.at[n]).start()
        else:
            cols = pl.ds(pl.multiple_of(swapped(which) * DH, DH), DH)
            pltpu.make_async_copy(wk_hbm.at[:, cols], w_v.at[n, :, pl.ds(0, DH)], load_sem.at[n]).start()
            pltpu.make_async_copy(wv_hbm.at[:, cols], w_v.at[n, :, pl.ds(DH, DH)], load_sem.at[n]).start()

    barrier = pltpu.get_barrier_semaphore()

    def greet(s, h):
        pl.semaphore_signal(barrier, inc=1, device_id=(s, h), device_id_type=MESH)

    for i in range(4):
        @pl.when(jnp.logical_not(jnp.logical_and(straight, z == i)))
        def _():
            greet(seq_of(core, x, i), y_hi * 2 + y_lo)
    for s, h in ((x_up, head), (x_down, head), (z_up, head), (z_down, head),
                 (seq, sib), (y_seq, head), (y_seq, cross_head)):
        greet(s, h)

    for hi in range(2):
        for lo in range(2):
            for zz in range(4):
                same = functools.reduce(jnp.logical_and, (straight, y_hi == hi, y_lo == lo, z == zz))

                @pl.when(jnp.logical_not(same))
                def _(hi=hi, lo=lo, zz=zz):
                    greet(seq_of(lo, x, zz), hi * 2 + y_lo)
    flag_peers = [(seq_of((y_lo + n // 4) % 2, x, (z + n) % 4), head) for n in range(1, 8)] + [
        (seq_of(y_lo, (x + n) % 4, z), head) for n in range(1, 4)
    ] + [(seq, (head + n) % 4) for n in range(1, 4)]
    for s, h in flag_peers:
        greet(s, h)

    lane = lax.broadcasted_iota(jnp.int32, (1, DH), 1)
    frequency = jnp.exp((lane % (DH // 2)).astype(F32) * (-2.0 * math.log(500000.0) / DH))
    sign = jnp.where(lane < DH // 2, -1.0, 1.0)

    def angle_rows(n, _):
        rows = pl.ds(pl.multiple_of(n * 64, 64), 64)
        position = (lax.broadcasted_iota(jnp.int32, (64, DH), 0) + (seq * rows_here + n * 64)).astype(F32)
        angle = position * frequency
        cos_v[rows, :] = jnp.cos(angle)
        sin_v[rows, :] = jnp.sin(angle) * sign
        return 0

    lax.fori_loop(0, rows_here // 64, angle_rows, 0)

    def w_chunk(colour_y, colour_z, q):
        base = (colour_y * 2 + colour_z) * 128 + 32 * (q % 4)
        return pl.ds(pl.multiple_of(base, 32), 32)

    def w_rows(q, y=None, z_par=None):
        y = y_lo if y is None else y
        z_par = z % 2 if z_par is None else z_par
        return w_chunk(y if q < 4 else 1 - y, z_par, q)

    group = (1 - y_hi) * 2 + core

    def w_cross(n):
        q = CROSS[n]
        rows = w_rows(q, y=1 - y_lo) if q < 8 else w_rows(q - 8, y=1 - y_lo, z_par=1 - z % 2)
        return remote(wo_hbm.at[rows], w_full.at[head, rows], wx_send.at[n], wx_recv.at[CROSS[n]], y_seq, cross_head)

    def w_y(q):
        rows = w_rows(q)
        return remote(w_full.at[group, rows], w_full.at[group, rows], wy_send.at[q], wx_recv.at[q + 4], y_seq, head)

    def w_z(q, rows=None):
        rows = w_rows(q) if rows is None else rows
        return remote(w_full.at[group, rows], w_full.at[group, rows], wz_send.at[q], wz_recv.at[q],
                      z_up if q % 2 == 0 else z_down, head)

    def w_sib(n):
        if n == 16:
            return remote(wo_hbm, w_full.at[head], ws_send.at[16], ws_recv.at[16], seq, sib)
        rows = w_rows(n) if n < 8 else w_rows(n - 8, z_par=1 - z % 2)
        return remote(w_full.at[group, rows], w_full.at[group, rows], ws_send.at[n], ws_recv.at[n], seq, sib)

    def w_arrived(q):
        rows = w_rows(q)
        remote(w_full.at[group, rows], w_full.at[group, rows], wx_send.at[0], wx_recv.at[q], y_seq, head).wait_recv()
        if q < 2:
            w_y(q).start()
        if q + 8 not in CROSS:
            w_z(q).start()
        w_sib(q).start()

    def w_side(q):
        if q + 8 in CROSS:
            rows = w_rows(q, z_par=1 - z % 2)
            remote(w_full.at[group, rows], w_full.at[group, rows], wx_send.at[0], wx_recv.at[q + 8], y_seq, head).wait_recv()
            w_sib(8 + q).start()
            return
        w_z(q, w_rows(q, z_par=1 - z % 2)).wait_recv()
        w_sib(8 + q).start()

    own_w = pltpu.make_async_copy(wo_hbm, w_full.at[head], load_sem.at[7])

    flag_cols = jnp.broadcast_to(flags_ref[...].astype(F32), (DH, rows_here)).T
    width = tok_v.shape[1]
    tok_v[rows_here:, :] = jnp.broadcast_to(embed_ref[...].reshape(1, width), (16, width))
    tok_load.wait()

    def rope(rows):
        return rows * cos_v[...] + pltpu.roll(rows, DH // 2, 1) * sin_v[...]

    def q_piece(m, i):
        return (remote(stq.at[m], qb.at[z], q_send.at[m], q_recv.at[z], seq_of(core, x, i), y_hi * 2 + y_lo),
                pltpu.make_async_copy(stq.at[m], qb.at[z], q_recv.at[z]))

    def kv_piece(high, low, i):
        slot = (1 - high) * low * OWN[0, 1] + high * (OWN[0, 2] + low * (OWN[0, 3] - OWN[0, 2]))
        m = 2 * high + low
        return (remote(stkv.at[m], kvb.at[slot], a_send.at[m], kv_recv.at[slot],
                       seq_of(core, x, i), y_hi * 2 + y_lo),
                pltpu.make_async_copy(stkv.at[m], kvb.at[slot], kv_recv.at[slot]))

    def launch(there, here, i):
        own = jnp.logical_and(straight, z == i)
        pl.when(own)(here.start)
        pl.when(jnp.logical_not(own))(there.start)

    def among(n, picks):
        return functools.reduce(jnp.logical_or, [n == p for p in picks])

    crooked = jnp.logical_not(straight)
    sends = {}

    def forward(slot, to_slot, s, h, only=None):
        n_send = sends.setdefault((slot, to_slot), (len(sends), s, h, only))[0]
        copy = remote(kvb.at[slot], kvb.at[to_slot], f_send.at[n_send], kv_recv.at[to_slot], s, h)
        if only is None:
            copy.start()
        else:
            pl.when(only)(copy.start)

    def take_up(slot):
        remote(kvb.at[slot], kvb.at[slot], f_send.at[0], kv_recv.at[slot], seq, sib).wait_recv()
        if slot not in OWN_OF:
            return
        dx, d = OWN_OF[slot]
        if dx == 0:
            forward(slot, OWN[1, d], x_up, head)
            forward(slot, OWN[3, d], x_down, head)
        if dx == 1:
            forward(slot, OWN[2, d], x_up, head, straight if d in (0, 3) else crooked)
        if dx == 3:
            forward(slot, OWN[2, d], x_down, head, crooked if d in (0, 3) else straight)
        forward(slot, SIB[dx, d], seq, sib)

    taken = set()

    def arrived(slot, kind=None):
        if slot in taken:
            return
        if kind is None:
            taken.add(slot)
            take_up(slot)
        else:
            if kind == "crooked":
                taken.add(slot)
            pl.when(straight if kind == "straight" else crooked)(functools.partial(take_up, slot))

    score_scale = DH ** -0.5 * math.log2(math.e)
    q_steps = [n for n, (kind, _) in enumerate(ORDER) if kind == "q"]
    kv_steps = {e: n for n, (kind, e) in enumerate(ORDER) if kind == "kv"}

    def project(n, _):
        pltpu.make_async_copy(wq_hbm.at[:, pl.ds(0, 256)], w_v.at[n], load_sem.at[n]).wait()
        pacc[...] = jnp.dot(tok_v[...], w_v[n], preferred_element_type=F32)

        @pl.when(n == 0)
        def _():
            @pl.when(straight)
            def _():
                pl.semaphore_wait(barrier, 38)

            @pl.when(jnp.logical_not(straight))
            def _():
                pl.semaphore_wait(barrier, 40)

            for k in range(len(CROSS)):
                w_cross(k).start()

        @pl.when(jnp.logical_or(jnp.logical_and(straight, n == 1), jnp.logical_and(crooked, n == 3)))
        def _():
            taken.add(OWN[0, 0])
            take_up(OWN[0, 0])

        def rows(e):
            cols = slice(e * DH, (e + 1) * DH)
            return pacc[0:rows_here, cols] + flag_cols * pacc[rows_here:rows_here + 1, cols]

        @pl.when(among(n, q_steps))
        def _():
            apart = n - q_steps[0]
            for e in range(2):
                i = (z // 2 + apart) % 2 * 2 + e
                m = apart * 2 + e
                stq[m] = turned_blocks((rope(rows(e)) * score_scale).astype(BF16))
                launch(*q_piece(m, i), i)

        @pl.when(jnp.logical_not(among(n, q_steps)))
        def _():
            high = among(n, (kv_steps[2], kv_steps[3])).astype(jnp.int32)
            low = among(n, (kv_steps[1], kv_steps[3])).astype(jnp.int32)
            i = (z // 2 + high) % 2 * 2 + (z + low) % 2
            m = 2 * high + low
            stkv[m, 0] = rope(rows(0)).astype(BF16)
            stkv[m, 1] = turned_blocks(rows(1).astype(BF16))

            @pl.when(jnp.logical_or(high == 0, straight))
            def _():
                launch(*kv_piece(high, low, i), i)
        return 0

    lax.fori_loop(0, 6, project, 0)

    acc[...] = jnp.zeros_like(acc)
    total_v[...] = jnp.zeros_like(total_v)
    for key in ((1, 0), (3, 0)):
        arrived(OWN[key])
    for j in range(4):
        remote(qb.at[j], qb.at[j], q_send.at[0], q_recv.at[j], seq, sib).wait_recv()
    own_w.start()
    pl.when(crooked)(kv_piece(1, 1, swapped(3))[0].start)
    blocks = qb.shape[0]

    def take(k):
        if k == 1:
            pl.when(crooked)(kv_piece(1, 0, swapped(2))[0].start)
        for dx, e, kind in EARLY.get(k, ()):
            arrived(OWN[dx, e], kind)
        arrived(2 * k)
        arrived(2 * k + 1)
        for action, n in EXTRA.get(k, ()):
            if action == "own":
                w_sib(16).start()
            elif action == "in":
                w_arrived(n)
            else:
                w_side(n)

    def chunk_pair(t):
        keys = kvb[pl.ds(2 * t, 2), 0].reshape(1024, DH)
        return keys, lanes(kvb[pl.ds(2 * t, 2), 1].reshape(8, DH, DH))

    def scores(keys, i):
        return jnp.dot(keys, lanes(qb[i].reshape(4, DH, DH)), preferred_element_type=F32)

    def add_weighted(now, values, cols):
        weights = jnp.exp2(now)
        total_v[:, cols] += jnp.sum(weights.reshape(128, 8, 512), axis=0)
        acc[:, cols] += jnp.dot(values, weights.astype(BF16), preferred_element_type=F32)

    def step(t, _):
        for k in range(LAST):
            pl.when(t == k)(functools.partial(take, k))
        keys, values = chunk_pair(t)
        now = scores(keys, 0)
        for i in range(blocks):
            later = scores(keys, i + 1) if i + 1 < blocks else None
            add_weighted(now, values, slice(i * 512, (i + 1) * 512))
            now = later
        return 0

    lax.fori_loop(0, LAST, step, 0)
    for k in range(LAST, 16):
        take(k)

    mine = y_hi * 8 + y_lo * 4 + z

    def o_piece(zz, hi, c):
        rows = pl.ds(pl.multiple_of(zz * 512 + hi * 256 + c * 128, 128), 128)
        return (remote(o_v.at[rows], full.at[mine], o_send.at[zz * 4 + hi * 2 + c], o_recv.at[mine],
                       seq_of(core, x, zz), hi * 2 + c),
                pltpu.make_async_copy(o_v.at[rows], full.at[mine], o_recv.at[mine]))

    def o_stays(zz, hi, c):
        return functools.reduce(jnp.logical_and, (straight, zz == z, y_hi == hi, core == c))

    def last(n, _):
        zz = (z + block_order(n)) % 4
        cols = pl.ds(pl.multiple_of(zz * 512, 512), 512)
        pairs = [chunk_pair(t) for t in range(LAST, 16)]
        now = scores(pairs[0][0], zz)
        for k, (_, values) in enumerate(pairs):
            later = scores(pairs[k + 1][0], zz) if k + 1 < len(pairs) else None
            add_weighted(now, values, cols)
            now = later
        total = jnp.sum(total_v[:, cols], axis=0, keepdims=True)
        done = (acc[:, cols] / total).astype(BF16)
        for m in range(4):
            o_v[pl.ds(pl.multiple_of(zz * 512 + m * DH, DH), DH), :] = done[:, m * DH:(m + 1) * DH].T
        for hi in range(2):
            for c in range(2):
                there, here = o_piece(zz, hi, c)
                stays = o_stays(zz, hi, c)
                pl.when(stays)(here.start)
                pl.when(jnp.logical_not(stays))(there.start)
        return 0

    lax.fori_loop(0, blocks, last, 0)

    rounds = (range(0, 7), range(7, 10), range(10, 13))

    def flag(n):
        k = [n in r for r in rounds].index(True)
        return remote(flag_v.at[13 + k], flag_v.at[n], flag_send.at[n], flag_recv.at[n], *flag_peers[n])

    def tell(k):
        for n in rounds[k]:
            flag(n).start()

    def hear(k):
        for n in rounds[k]:
            flag(n).wait_recv()
        told = flag_v[13 + k]
        for n in rounds[k]:
            told = jnp.maximum(told, flag_v[n])
        return told

    sums = jnp.sum(total_v[...], axis=0, keepdims=True)
    good = jnp.logical_and(sums > TOTAL_LOW, sums < TOTAL_HIGH)
    flag_v[13] = jnp.broadcast_to(jnp.max(jnp.where(good, 0.0, 1.0), axis=1, keepdims=True), (8, DH))
    tell(0)
    for action, n in EXTRA[16]:
        w_arrived(n) if action == "in" else w_side(n)
    own_w.wait()
    for n in range(17):
        w_sib(n).wait_recv()

    def project_out(n, _):
        zz = (z + 4 - block_order(n)) % 4
        for hi in range(4):
            remote(full.at[hi * 4 + zz], full.at[hi * 4 + zz], o_send.at[0], o_recv.at[hi * 4 + zz], seq, sib).wait_recv()
        attention = jnp.concatenate([full[hi * 4 + zz] for hi in range(4)], axis=1)
        depth = pl.ds(pl.multiple_of(zz * DH, DH), DH)

        def columns(m, _):
            cols = pl.ds(pl.multiple_of(m * 512, 512), 512)
            weights = jnp.concatenate([w_full[hi, depth, cols] for hi in range(4)], axis=0)
            out_acc[:, cols] += jnp.dot(attention, weights, preferred_element_type=F32)
            return 0

        lax.fori_loop(0, out_ref.shape[1] // 512, columns, 0)
        for k in range(2):
            @pl.when(n == k)
            def _(k=k):
                flag_v[14 + k] = hear(k)
                tell(k + 1)
        return 0

    out_acc[...] = jnp.zeros_like(out_acc)
    lax.fori_loop(0, 4, project_out, 0)
    out_ref[...] = out_acc[...].astype(BF16)
    bad_ref[0, 0] = jnp.max(hear(2))

    for n in range(13):
        flag(n).wait_send()
    for zz in range(4):
        for hi in range(2):
            for c in range(2):
                pl.when(jnp.logical_not(o_stays(zz, hi, c)))(o_piece(zz, hi, c)[0].wait_send)
    for n in range(17):
        w_sib(n).wait_send()
    for n in range(len(CROSS)):
        w_cross(n).wait_send()
    for q in range(2):
        w_y(q).wait_send()
    for q in range(8):
        if q + 8 not in CROSS:
            w_z(q).wait_send()
    for m in range(4):
        own = jnp.logical_and(straight, z % 2 == m) if m < 2 else None
        for there, alone in ((q_piece(m, 0)[0], own), (kv_piece(m // 2, m % 2, 0)[0], straight if m == 0 else None)):
            if alone is None:
                there.wait_send()
            else:
                pl.when(jnp.logical_not(alone))(there.wait_send)
    for (slot, to_slot), (n, s, h, only) in sends.items():
        copy = remote(kvb.at[slot], kvb.at[to_slot], f_send.at[n], kv_recv.at[to_slot], s, h)
        if only is None:
            copy.wait_send()
        else:
            pl.when(only)(copy.wait_send)


def rotate(values, positions, head_size):
    halfway = head_size // 2
    indices = jnp.arange(halfway).astype(jnp.float32)
    frequency = jnp.exp(indices * (-2.0 * math.log(500000.0) / head_size))
    angles = positions[:, None] * frequency[None, :]
    cosine = jnp.cos(angles)[:, None, :]
    sine_table = jnp.sin(angles)[:, None, :]
    shaped = values.reshape(values.shape[0], -1, head_size)
    leading = shaped[..., :halfway]
    trailing = shaped[..., halfway:]
    turned = jnp.concatenate(
        [leading * cosine - trailing * sine_table, trailing * cosine + leading * sine_table],
        axis=-1,
    )
    return turned.reshape(values.shape)


def plain_shards(tokens, mask_flags, mask_embed, w_query, w_key, w_value, w_out):
    tok_rows = tokens.shape[0]
    head_size = DH
    heads_here = w_query.shape[1] // head_size
    mask_rows = mask_flags.astype(jnp.float32)[:, None]
    hidden = (
        tokens.astype(jnp.float32) + mask_rows * mask_embed.astype(jnp.float32)[None, :]
    ).astype(jnp.bfloat16)
    positions = (lax.axis_index("seq") * tok_rows + jnp.arange(tok_rows)).astype(jnp.float32)
    query_rows = rotate(
        jnp.dot(hidden, w_query, preferred_element_type=jnp.float32), positions, head_size
    ).astype(jnp.bfloat16)
    key_rows = rotate(
        jnp.dot(hidden, w_key, preferred_element_type=jnp.float32), positions, head_size
    ).astype(jnp.bfloat16)
    value_rows = jnp.dot(hidden, w_value, preferred_element_type=jnp.float32).astype(jnp.bfloat16)
    queries = query_rows.reshape(tok_rows, heads_here, head_size)
    score_scale = head_size ** (-0.5)
    row_peak = jnp.full((heads_here, tok_rows), -1e30, jnp.float32)
    weighted = jnp.zeros((tok_rows, heads_here, head_size), jnp.float32)
    peers = lax.axis_size("seq")
    ring = [(n, (n + 1) % peers) for n in range(peers)]

    def add_part(_, carried):
        keys, values, row_peak, total, weighted = carried
        scores = (
            jnp.einsum("qhd,khd->hqk", queries, keys.reshape(queries.shape), preferred_element_type=jnp.float32)
            * score_scale
        )
        new_peak = jnp.maximum(row_peak, jnp.max(scores, axis=-1))
        factor = jnp.exp(row_peak - new_peak)
        weights = jnp.exp(scores - new_peak[..., None])
        total = total * factor + jnp.sum(weights, axis=-1)
        update = jnp.einsum(
            "hqk,khd->qhd", weights.astype(jnp.bfloat16), values.reshape(queries.shape), preferred_element_type=jnp.float32
        )
        weighted = weighted * factor.T[:, :, None] + update
        return lax.ppermute(keys, "seq", ring), lax.ppermute(values, "seq", ring), new_peak, total, weighted

    _, _, _, total, weighted = lax.fori_loop(
        0, peers, add_part, (key_rows, value_rows, row_peak, jnp.zeros_like(row_peak), weighted)
    )
    attention = (weighted / total.T[:, :, None]).reshape(tok_rows, heads_here * head_size).astype(jnp.bfloat16)
    partials = jnp.dot(attention, w_out, preferred_element_type=jnp.float32)
    heads = lax.axis_size("head")
    here, part = lax.axis_index("head"), tok_rows // heads
    mixed_rows = lax.dynamic_slice_in_dim(partials, here * part, part, 0)
    for n in range(1, heads):
        leaving = lax.dynamic_slice_in_dim(partials, (here + n) % heads * part, part, 0)
        mixed_rows += lax.ppermute(leaving, "head", [(m, (m + n) % heads) for m in range(heads)])
    return mixed_rows.astype(jnp.bfloat16)


def shards(tokens, mask_flags, mask_embed, w_query, w_key, w_value, w_out):
    rows, width = tokens.shape
    vmem, hbm = pl.BlockSpec(memory_space=pltpu.VMEM), pl.BlockSpec(memory_space=pl.ANY)
    dma = pltpu.SemaphoreType.DMA
    struct = jax.ShapeDtypeStruct
    mixed_rows, bad = pl.pallas_call(
        attend_kernel,
        out_shape=(struct((rows // 4, width), BF16), struct((1, 1), F32)),
        in_specs=[hbm, vmem, vmem, hbm, hbm, hbm, hbm],
        out_specs=(vmem, pl.BlockSpec(memory_space=pltpu.SMEM)),
        scratch_shapes=[
            pltpu.VMEM((rows + 16, width), BF16),
            pltpu.VMEM((6, width, 256), BF16),
            pltpu.VMEM((rows + 16, 256), F32),
            pltpu.VMEM((rows, DH), F32),
            pltpu.VMEM((rows, DH), F32),
            pltpu.VMEM((4, rows, DH), BF16),
            pltpu.VMEM((4, 2, rows, DH), BF16),
            pltpu.VMEM((4, rows, DH), BF16),
            pltpu.VMEM((32, 2, rows, DH), BF16),
            pltpu.VMEM((DH, 4 * rows), F32),
            pltpu.VMEM((8, 4 * rows), F32),
            pltpu.VMEM((4 * rows, DH), BF16),
            pltpu.VMEM((16, DH, DH), BF16),
            pltpu.VMEM((4,) + w_out.shape, BF16),
            pltpu.VMEM((16, 8, DH), F32),
            pltpu.VMEM((rows // 4, width), F32),
            dma((8,)), dma((4,)), dma((4,)), dma((4,)), dma((32,)), dma((32,)),
            dma((7,)), dma((2,)), dma((16,)), dma((8,)), dma((8,)), dma((17,)), dma((17,)),
            dma((16,)), dma((16,)), dma((13,)), dma((13,)),
        ],
        compiler_params=pltpu.CompilerParams(
            collective_id=0, has_side_effects=True, vmem_limit_bytes=VMEM_BYTES
        ),
        name="attend",
    )(tokens, mask_flags.reshape(1, rows), mask_embed, w_query, w_key, w_value, w_out)
    return lax.cond(
        bad[0, 0] > 0.5,
        lambda: plain_shards(tokens, mask_flags, mask_embed, w_query, w_key, w_value, w_out),
        lambda: mixed_rows,
    )


def solution(mesh):
    placed = (
        P("seq", None),
        P("seq"),
        P(),
        P(None, "head"),
        P(None, "head"),
        P(None, "head"),
        P("head", None),
    )
    return jax.shard_map(
        shards, mesh=mesh, in_specs=placed, out_specs=P(("seq", "head"), None), check_vma=False
    )
```
